512 devices in a mesh: hst: 32 (over y, x, core), tp: 16 (over z).
Axes of the slice: x: 4, y: 4, z: 16, core: 2. Of those that a mesh axis runs over, the one named last changes fastest.
Arguments:
- ctx_q: bfloat16 [24576, 8192], P('hst', 'tp'), may hold values from -11.2 to 11.2
- ctx_kv: bfloat16 [2, 24576, 1024], P(None, 'hst'), may hold values from -4.5 to 4.5
- lengths: int32 [32], replicated, may hold values from 192 to 768, as said below
- query_q: bfloat16 [64, 8192], P('hst', 'tp'), may hold values from -11.2 to 11.2
- query_kv: bfloat16 [2, 64, 1024], P(None, 'hst'), may hold values from -4.5 to 4.5
- out_weight: bfloat16 [8192, 8192], P('tp', 'hst'), may hold values from -0.0625 to 0.0625
Outputs:
- context_out: bfloat16 [24576, 8192], P('hst', 'tp')
- query_out: bfloat16 [64, 8192], P(None, 'hst')
The draws below stay inside these ranges and needn't reach their ends.
Inputs may be any that keep to these rules, and one draw needn't show every extreme that they name: lengths[0] is 768; blocks with index below three quarters of 32 are full, the last block holds 192 live positions.
All inputs are finite; a program needn't handle non-finite values.
Results may differ from the reference program's by a relative error of at most 0.012.
Values may be sent and summed in bfloat16 or wider, within the bound.
A program may use at most 64 MiB of HBM per device.

```python
import jax
import jax.numpy as jnp
from jax import lax

D = 8192
H = 64
KVH = 8
HD = 128
SLAB = 768
QN = 64
TOKENS = 24576
N_HST = 32


def draw_ctx_q(key, part):
    key = jax.random.fold_in(key, 1)
    full_shape = (TOKENS, H, HD)
    result = jnp.clip(2.8 * jax.random.normal(key, full_shape, jnp.float32), -11.2, 11.2)
    return result.reshape(TOKENS, H * HD).astype(jnp.bfloat16)


def draw_ctx_kv(key, part):
    key = jax.random.fold_in(key, 2)
    key_draw, value_draw = jax.random.split(key)
    full_shape = (TOKENS, KVH, HD)
    key_rows = jnp.clip(jax.random.normal(key_draw, full_shape, jnp.float32), -4.5, 4.5)
    value_rows = jnp.clip(jax.random.normal(value_draw, full_shape, jnp.float32), -4.5, 4.5)
    stacked = jnp.stack([key_rows, value_rows], 0)
    return stacked.reshape(2, TOKENS, KVH * HD).astype(jnp.bfloat16)


def draw_lengths(key, part):
    key = jax.random.fold_in(key, 5)
    host_count = TOKENS // SLAB
    host_ids = jnp.arange(host_count)
    random_len = jax.random.randint(key, (host_count,), SLAB // 4, SLAB + 1)
    result = jnp.where(host_ids * 4 < host_count * 3, SLAB, random_len)
    return jnp.where(host_ids == host_count - 1, SLAB // 4, result).astype(jnp.int32)


def draw_query_q(key, part):
    key = jax.random.fold_in(key, 3)
    full_shape = (QN, H, HD)
    result = jnp.clip(2.8 * jax.random.normal(key, full_shape, jnp.float32), -11.2, 11.2)
    return result.reshape(QN, H * HD).astype(jnp.bfloat16)


def draw_query_kv(key, part):
    key = jax.random.fold_in(key, 4)
    full_shape = (2, QN, KVH * HD)
    result = jnp.clip(jax.random.normal(key, full_shape, jnp.float32), -4.5, 4.5)
    return result.astype(jnp.bfloat16)


def levels(key, extent, pieces, low, largest):
    factor_of = 1.0
    for axis_at, parts in pieces:
        draws = jax.random.uniform(jax.random.fold_in(jax.random.fold_in(key, 6), axis_at), (parts,), jnp.float32, low / len(pieces), largest / len(pieces))
        factor_of = factor_of * jnp.repeat(jnp.exp(draws), extent[axis_at] // parts).reshape((-1,) + (1,) * (len(extent) - 1 - axis_at))
    return factor_of


def noise(rng, shape, spread, bound, cuts=(), held_as=jnp.bfloat16):
    loudness = levels(rng, shape, cuts, -0.22, 0.18) if cuts else 1.0
    entries = jax.random.normal(rng, shape, jnp.float32) * spread * loudness
    return jnp.minimum(jnp.maximum(entries, -bound), bound).astype(held_as)


def setup_inputs(seed: int = 0) -> dict:
    key_list = jax.random.split(jax.random.key(seed), 7)
    return {
        "ctx_q": draw_ctx_q(jax.random.fold_in(key_list[6], 71), 0),
        "ctx_kv": draw_ctx_kv(jax.random.fold_in(key_list[6], 71), 0),
        "lengths": draw_lengths(jax.random.fold_in(key_list[6], 71), 0),
        "query_q": draw_query_q(jax.random.fold_in(key_list[6], 71), 0),
        "query_kv": draw_query_kv(jax.random.fold_in(key_list[6], 71), 0),
        "out_weight": noise(key_list[5], (H * HD, D), (H * HD) ** -0.5, 0.0625, ((0, 16), (1, 32))),
    }


MASKED = -1.0e30


def reference(ctx_q, ctx_kv, lengths, query_q, query_kv, out_weight):
    group_size = H // KVH
    score_scale = HD ** -0.5
    q_rows = QN // N_HST
    row_ids = jnp.arange(SLAB)
    query_ids = jnp.arange(QN)
    block_q = ctx_q.reshape(N_HST, SLAB, H, HD)
    block_k = ctx_kv[0].reshape(N_HST, SLAB, KVH, HD)
    block_v = ctx_kv[1].reshape(N_HST, SLAB, KVH, HD)
    anchor_k = block_k[0]
    anchor_v = block_v[0]
    first_len = lengths[0]

    def encode_block(operands):
        host_id, q_block, k_block, v_block, own_len = operands
        own_ok = (row_ids[None, :] <= row_ids[:, None]) & (row_ids[None, :] < own_len)
        anchor_ok = (row_ids[None, :] < first_len) & (host_id > 0)
        allowed = jnp.concatenate([jnp.broadcast_to(anchor_ok, (SLAB, SLAB)), own_ok], 1)
        key_rows = jnp.concatenate([anchor_k, k_block], 0).transpose(1, 0, 2)
        value_rows = jnp.concatenate([anchor_v, v_block], 0).transpose(1, 0, 2)

        def per_group(inner):
            query_group, key_group, value_group = inner
            scores = jnp.einsum("igd,jd->gij", query_group.astype(jnp.float32), key_group.astype(jnp.float32)) * score_scale
            scores = jnp.where(allowed[None], scores, MASKED)
            peak = jnp.max(scores, axis=2, keepdims=True)
            expo = jnp.exp(scores - peak)
            probs = (expo / jnp.sum(expo, axis=2, keepdims=True)).astype(jnp.bfloat16)
            encoded = jnp.einsum("gij,jd->igd", probs.astype(jnp.float32), value_group.astype(jnp.float32))
            return encoded.astype(jnp.bfloat16)

        grouped = q_block.reshape(SLAB, KVH, group_size, HD).transpose(1, 0, 2, 3)
        encoded = lax.map(per_group, (grouped, key_rows, value_rows))
        encoded = encoded.transpose(1, 0, 2, 3).reshape(SLAB, H * HD)
        return jnp.where((row_ids < own_len)[:, None], encoded, jnp.zeros_like(encoded))

    context_out = lax.map(encode_block, (jnp.arange(N_HST), block_q, block_k, block_v, lengths))
    context_out = context_out.reshape(TOKENS, H * HD)

    query_groups = query_q.reshape(QN, KVH, group_size, HD).transpose(1, 0, 2, 3)
    self_k = query_kv[0].reshape(N_HST, q_rows, KVH, HD)
    self_v = query_kv[1].reshape(N_HST, q_rows, KVH, HD)

    def score_source(operands):
        host_id, k_block, v_block, own_len, self_keys, self_values = operands
        key_rows = jnp.concatenate([k_block, self_keys], 0).transpose(1, 0, 2)
        value_rows = jnp.concatenate([v_block, self_values], 0).transpose(1, 0, 2)
        context_ok = jnp.broadcast_to(row_ids[None, :] < own_len, (QN, SLAB))
        self_ok = (host_id * q_rows + jnp.arange(q_rows))[None, :] <= query_ids[:, None]
        allowed = jnp.concatenate([context_ok, self_ok], 1)

        def per_group(inner):
            query_group, key_group, value_group = inner
            scores = jnp.einsum("igd,jd->gij", query_group.astype(jnp.float32), key_group.astype(jnp.float32)) * score_scale
            scores = jnp.where(allowed[None], scores, MASKED)
            peak = jnp.max(scores, axis=2)
            expo = jnp.exp(scores - peak[:, :, None])
            denominator = jnp.sum(expo, axis=2)
            weighted = jnp.einsum("gij,jd->gid", expo.astype(jnp.bfloat16).astype(jnp.float32), value_group.astype(jnp.float32))
            return peak, denominator, weighted

        peak, denominator, weighted = lax.map(per_group, (query_groups, key_rows, value_rows))
        return peak.reshape(H, QN), denominator.reshape(H, QN), weighted.reshape(H, QN, HD)

    maxima, totals, outputs = lax.map(score_source, (jnp.arange(N_HST), block_k, block_v, lengths, self_k, self_v))
    global_max = jnp.max(maxima, axis=0)
    factor = jnp.exp(maxima - global_max[None])
    denominator = jnp.sum(totals * factor, axis=0)
    summed = jnp.sum(outputs * factor[..., None], axis=0)
    attended = (summed / denominator[..., None]).astype(jnp.bfloat16)
    attended = attended.transpose(1, 0, 2).reshape(QN, H * HD)
    query_out = jnp.dot(attended, out_weight, preferred_element_type=jnp.float32).astype(jnp.bfloat16)
    return context_out, query_out
```

```python
import jax
import jax.numpy as jnp
from jax import lax
from jax.experimental import pallas as pl
from jax.experimental.pallas import tpu as pltpu
from jax.sharding import PartitionSpec as P

H = 64
KVH = 8
HD = 128
HST = 32
TP = 16
ROWS = 768
HEADS = H // TP
TILE = 256
CHIPS = HST // 2
PIECE = ROWS // CHIPS
QN = 64
COLS = 256
MASKED = -1e30
SCALE2 = HD ** (-0.5) * 1.4426950408889634
MESH = pl.DeviceIdType.MESH


def dot_t(a, b):
    return lax.dot_general(a, b, (((1,), (1,)), ((), ())), preferred_element_type=jnp.float32)


def dot(a, b):
    return jnp.dot(a, b, preferred_element_type=jnp.float32)


def with_ones(values):
    return jnp.concatenate([values, jnp.ones_like(values)], axis=1)


def kernel(
    lengths,
    ctx_q,
    ctx_kv,
    query_q,
    query_kv,
    out_weight,
    ctx_out,
    query_out,
    cq,
    own,
    anchor,
    weight,
    qq,
    qkv,
    selfkv,
    out1,
    sum1,
    max1,
    enc,
    gather_q,
    rows_q,
    sent_b,
    got_b,
    att,
    part,
    got_d,
    got_e,
    qout,
    local_sem,
    out_sem,
    send_sem,
    recv_sem,
):
    me = lax.axis_index("hst")
    z = lax.axis_index("tp")
    chip = me // 2
    core = lax.rem(me, 2)
    kv_off = pl.multiple_of((z // 2) * HD, HD)

    def at_hst(d):
        return {"hst": d}

    def at_tp(d):
        return {"tp": d}

    load_kv = pltpu.make_async_copy(ctx_kv.at[:, :, pl.ds(kv_off, HD)], own, local_sem.at[0])
    load_cq = pltpu.make_async_copy(ctx_q, cq, local_sem.at[1])
    load_qq = pltpu.make_async_copy(query_q, qq, local_sem.at[2])
    load_qkv = pltpu.make_async_copy(query_kv, qkv, local_sem.at[3])
    load_w = pltpu.make_async_copy(out_weight, weight, local_sem.at[4])
    for copy in (load_qq, load_kv, load_cq, load_qkv, load_w):
        copy.start()

    barrier = pltpu.get_barrier_semaphore()

    @pl.loop(1, HST)
    def _(k):
        pl.semaphore_signal(
            barrier, inc=1, device_id=at_hst(lax.rem(me + k, HST)), device_id_type=MESH
        )

    @pl.loop(1, TP)
    def _(k):
        pl.semaphore_signal(
            barrier, inc=1, device_id=at_tp(lax.rem(z + k, TP)), device_id_type=MESH
        )

    own_len = lengths[me]

    diag_row = lax.broadcasted_iota(jnp.int32, (TILE, TILE), 0)
    diag_col = lax.broadcasted_iota(jnp.int32, (TILE, TILE), 1)

    def own_head(h):
        for rb in range(ROWS // TILE):
            rows = pl.ds(rb * TILE, TILE)
            q = cq[rows, h * HD : (h + 1) * HD]
            keys = (rb + 1) * TILE
            s = dot_t(q, own[0, 0:keys, :])
            last = jnp.where(diag_col <= diag_row, s[:, keys - TILE :], MASKED)
            s = last if rb == 0 else jnp.concatenate([s[:, : keys - TILE], last], axis=1)
            m = jnp.max(s, axis=1, keepdims=True) * SCALE2
            p = jnp.exp2(s * SCALE2 - m).astype(jnp.bfloat16)
            o = dot(p, with_ones(own[1, 0:keys, :]))
            out1[h, rows, :] = o[:, :HD]
            sum1[h, rows, :] = o[:, HD:]
            max1[h, rows, :] = jnp.broadcast_to(m, (TILE, HD))

    def live(rb, value):
        rid = rb * TILE + lax.broadcasted_iota(jnp.int32, (TILE, HD), 0)
        return jnp.where(rid < own_len, value, 0.0).astype(jnp.bfloat16)

    def anchor_head(h):
        for rb in range(ROWS // TILE):
            rows = pl.ds(rb * TILE, TILE)
            q = cq[rows, h * HD : (h + 1) * HD]
            s = dot_t(q, anchor[0])
            before = max1[h, rows, :]
            m = jnp.maximum(jnp.max(s, axis=1, keepdims=True) * SCALE2, before[:, :1])
            p = jnp.exp2(s * SCALE2 - m).astype(jnp.bfloat16)
            o = dot(p, with_ones(anchor[1]))
            keep = jnp.exp2(before - m)
            num = out1[h, rows, :] * keep + o[:, :HD]
            den = sum1[h, rows, :] * keep + o[:, HD:]
            enc[rows, h * HD : (h + 1) * HD] = live(rb, num / den)

    def first_head(h):
        for rb in range(ROWS // TILE):
            rows = pl.ds(rb * TILE, TILE)
            enc[rows, h * HD : (h + 1) * HD] = live(rb, out1[h, rows, :] / sum1[h, rows, :])

    def finish_head(h):
        @pl.when(me > 0)
        def _():
            anchor_head(h)

        @pl.when(me == 0)
        def _():
            first_head(h)

        pltpu.make_async_copy(
            enc.at[:, pl.ds(h * HD, HD)], ctx_out.at[:, pl.ds(h * HD, HD)], out_sem.at[h]
        ).start()

    load_qq.wait()
    mine = qq[...].astype(jnp.float32)
    gather_q[pl.ds(me, 1)] = jnp.concatenate(
        [mine[t : t + 1, h * HD : (h + 1) * HD] for t in range(2) for h in range(HEADS)], axis=0
    ).astype(jnp.bfloat16)[None]

    load_kv.wait()
    load_cq.wait()
    own_head(0)

    pl.semaphore_wait(barrier, HST - 1 + TP - 1)

    @pl.loop(1, HST)
    def _(k):
        pltpu.make_async_remote_copy(
            gather_q.at[me], gather_q.at[me], send_sem.at[0], recv_sem.at[0],
            device_id=at_hst(lax.rem(me + k, HST)), device_id_type=MESH,
        ).start()

    def piece(ref, plane, c):
        return ref.at[plane, pl.ds(pl.multiple_of(c * PIECE, 16), PIECE), :]

    @pl.when(me == 0)
    def _():
        @pl.loop(1, CHIPS)
        def _(c):
            pltpu.make_async_remote_copy(
                piece(own, 0, c), piece(anchor, 0, c), send_sem.at[1], recv_sem.at[1],
                device_id=at_hst(c * 2), device_id_type=MESH,
            ).start()
            pltpu.make_async_remote_copy(
                piece(own, 1, c), piece(anchor, 1, c), send_sem.at[2], recv_sem.at[1],
                device_id=at_hst(c * 2 + 1), device_id_type=MESH,
            ).start()

        pltpu.make_async_remote_copy(
            piece(own, 1, 0), piece(anchor, 1, 0), send_sem.at[2], recv_sem.at[1],
            device_id=at_hst(1), device_id_type=MESH,
        ).start()

        @pl.loop(1, CHIPS)
        def _(c):
            pltpu.make_async_remote_copy(
                piece(own, 0, 0), piece(anchor, 0, 0), send_sem.at[3], recv_sem.at[2],
                device_id=at_hst(c * 2), device_id_type=MESH,
            ).start()

        pltpu.make_async_remote_copy(
            own.at[0], anchor.at[0], send_sem.at[4], recv_sem.at[3],
            device_id=at_hst(1), device_id_type=MESH,
        ).start()

    own_head(1)
    own_head(2)

    @pl.when(me > 0)
    def _():
        pltpu.make_async_copy(
            piece(anchor, 0, 0), piece(anchor, 0, 0), recv_sem.at[1]
        ).wait()

        @pl.loop(1, CHIPS)
        def _(k):
            c = lax.rem(chip + k, CHIPS)

            @pl.when(c * 2 + core > 0)
            def _():
                pltpu.make_async_remote_copy(
                    piece(anchor, core, chip), piece(anchor, core, chip),
                    send_sem.at[3], recv_sem.at[2],
                    device_id=at_hst(c * 2 + core), device_id_type=MESH,
                ).start()

    pltpu.make_async_copy(
        gather_q.at[pl.ds(0, HST - 1)], gather_q.at[pl.ds(0, HST - 1)], recv_sem.at[0]
    ).wait()
    rows_q[...] = gather_q[...].astype(jnp.float32).reshape(HST * 8, HD)
    q_all = jnp.concatenate(
        [rows_q[pl.ds(h, QN, stride=HEADS), :] for h in range(HEADS)], axis=0
    ).astype(jnp.bfloat16)
    load_qkv.wait()
    for plane in range(2):
        tiny = qkv[plane, :, pl.ds(kv_off, HD)].astype(jnp.float32)
        selfkv[plane] = jnp.concatenate(
            [tiny, jnp.zeros((HD - 2, HD), jnp.float32)], axis=0
        ).astype(jnp.bfloat16)
    s_ctx = dot_t(q_all, own[0])
    s_ctx = jnp.where(
        lax.broadcasted_iota(jnp.int32, s_ctx.shape, 1) < own_len, s_ctx, MASKED
    )
    s_self = dot_t(q_all, selfkv[0])
    token = lax.rem(lax.broadcasted_iota(jnp.int32, s_self.shape, 0), QN)
    key = lax.broadcasted_iota(jnp.int32, s_self.shape, 1)
    s_self = jnp.where((key < 2) & (me * 2 + key <= token), s_self, MASKED)
    peak = jnp.maximum(
        jnp.max(s_ctx, axis=1, keepdims=True), jnp.max(s_self, axis=1, keepdims=True)
    )
    peak = (peak * SCALE2).astype(jnp.bfloat16).astype(jnp.float32)
    p_ctx = jnp.exp2(s_ctx * SCALE2 - peak).astype(jnp.bfloat16)
    p_self = jnp.exp2(s_self * SCALE2 - peak).astype(jnp.bfloat16)
    o = dot(p_ctx, with_ones(own[1])) + dot(p_self, with_ones(selfkv[1]))
    lane = lax.broadcasted_iota(jnp.int32, (HEADS * QN, HD), 1)
    stats = jnp.where(lane < HD // 2, jnp.broadcast_to(peak, (HEADS * QN, HD)), o[:, HD:])
    sent_b[...] = jnp.concatenate(
        [o[:, :HD].reshape(HST, 8, HD), stats.reshape(HST, 8, HD)], axis=1
    ).astype(jnp.bfloat16)

    @pl.loop(1, HST)
    def _(k):
        d = lax.rem(me + k, HST)
        pltpu.make_async_remote_copy(
            sent_b.at[d], got_b.at[me], send_sem.at[5], recv_sem.at[4],
            device_id=at_hst(d), device_id_type=MESH,
        ).start()

    got_b[pl.ds(me, 1)] = sent_b[pl.ds(me, 1)]

    own_head(3)

    @pl.when(me > 0)
    def _():
        pltpu.make_async_copy(
            anchor.at[0, pl.ds(0, ROWS - PIECE)], anchor.at[0, pl.ds(0, ROWS - PIECE)], recv_sem.at[2]
        ).wait()

    @pl.when(me > 1)
    def _():
        pltpu.make_async_remote_copy(
            anchor.at[core], anchor.at[core], send_sem.at[4], recv_sem.at[3],
            device_id=at_hst(me + 1 - 2 * core), device_id_type=MESH,
        ).start()

    pltpu.make_async_copy(
        got_b.at[pl.ds(0, HST - 1)], got_b.at[pl.ds(0, HST - 1)], recv_sem.at[4]
    ).wait()
    terms = got_b[...].astype(jnp.float32)
    value, stat = terms[:, :8], terms[:, 8:]
    turned = pltpu.roll(stat, HD // 2, 2)
    low = lax.broadcasted_iota(jnp.int32, stat.shape, 2) < HD // 2
    peaks = jnp.where(low, stat, turned)
    sums = jnp.where(low, turned, stat)
    factor = jnp.exp2(peaks - jnp.max(peaks, axis=0, keepdims=True))
    attended = jnp.sum(factor * value, axis=0) / jnp.sum(factor * sums, axis=0)
    att[pl.ds(me, 1)] = attended.astype(jnp.bfloat16)[None]

    @pl.loop(1, HST)
    def _(k):
        pltpu.make_async_remote_copy(
            att.at[me], att.at[me], send_sem.at[6], recv_sem.at[5],
            device_id=at_hst(lax.rem(me + k, HST)), device_id_type=MESH,
        ).start()

    @pl.when(me > 0)
    def _():
        pltpu.make_async_copy(anchor.at[0], anchor.at[0], recv_sem.at[3]).wait()

    finish_head(0)

    load_w.wait()
    pltpu.make_async_copy(
        att.at[pl.ds(0, HST - 1)], att.at[pl.ds(0, HST - 1)], recv_sem.at[5]
    ).wait()
    rows = att[...].astype(jnp.float32).reshape(HEADS, QN, HD)
    wide = jnp.concatenate([rows[h] for h in range(HEADS)], axis=1).astype(jnp.bfloat16)
    partial = dot(wide, weight[...])
    for t in range(TP):
        r, c = t // 2, t % 2
        part[t] = partial[r * 8 : r * 8 + 8, c * HD : (c + 1) * HD].astype(jnp.bfloat16)

    @pl.loop(1, TP)
    def _(k):
        d = lax.rem(z + k, TP)
        pltpu.make_async_remote_copy(
            part.at[d], got_d.at[z], send_sem.at[7], recv_sem.at[6],
            device_id=at_tp(d), device_id_type=MESH,
        ).start()

    got_d[pl.ds(z, 1)] = part[pl.ds(z, 1)]
    finish_head(1)

    pltpu.make_async_copy(
        got_d.at[pl.ds(0, TP - 1)], got_d.at[pl.ds(0, TP - 1)], recv_sem.at[6]
    ).wait()
    total = jnp.sum(got_d[...].astype(jnp.float32), axis=0)
    got_e[pl.ds(z, 1)] = total.astype(jnp.bfloat16)[None]

    @pl.loop(1, TP)
    def _(k):
        pltpu.make_async_remote_copy(
            got_e.at[z], got_e.at[z], send_sem.at[8], recv_sem.at[7],
            device_id=at_tp(lax.rem(z + k, TP)), device_id_type=MESH,
        ).start()

    finish_head(2)
    finish_head(3)

    pltpu.make_async_copy(
        got_e.at[pl.ds(0, TP - 1)], got_e.at[pl.ds(0, TP - 1)], recv_sem.at[7]
    ).wait()
    tiles = got_e[...].astype(jnp.float32)
    qout[...] = jnp.concatenate(
        [
            jnp.concatenate([tiles[2 * r], tiles[2 * r + 1]], axis=1)
            for r in range(TP // 2)
        ],
        axis=0,
    ).astype(jnp.bfloat16)
    save_q = pltpu.make_async_copy(qout, query_out, local_sem.at[5])
    save_q.start()

    for sem, ref in (
        (0, gather_q.at[pl.ds(0, HST - 1)]),
        (5, got_b.at[pl.ds(0, HST - 1)]),
        (6, att.at[pl.ds(0, HST - 1)]),
        (7, got_d.at[pl.ds(0, TP - 1)]),
        (8, got_e.at[pl.ds(0, TP - 1)]),
    ):
        pltpu.make_async_copy(ref, ref, send_sem.at[sem]).wait()

    def sent(sem, rows):
        ref = own.at[0, pl.ds(0, rows)]
        pltpu.make_async_copy(ref, ref, send_sem.at[sem]).wait()

    @pl.when(me == 0)
    def _():
        sent(1, ROWS - PIECE)
        sent(2, ROWS)

    @pl.when(core + (me == 0) > 0)
    def _():
        sent(3, ROWS - PIECE)

    @pl.when(core + (me == 0) == 0)
    def _():
        sent(3, ROWS - 2 * PIECE)

    @pl.when((me == 0) | (me > 1))
    def _():
        sent(4, ROWS)

    save_q.wait()
    for h in range(HEADS):
        pltpu.make_async_copy(
            enc.at[:, pl.ds(h * HD, HD)], ctx_out.at[:, pl.ds(h * HD, HD)], out_sem.at[h]
        ).wait()


def per_device(ctx_q, ctx_kv, lengths, query_q, query_kv, out_weight):
    bf16, f32 = jnp.bfloat16, jnp.float32
    any_space = pl.BlockSpec(memory_space=pl.ANY)
    return pl.pallas_call(
        kernel,
        out_shape=(
            jax.ShapeDtypeStruct((ROWS, HEADS * HD), bf16),
            jax.ShapeDtypeStruct((QN, COLS), bf16),
        ),
        in_specs=[pl.BlockSpec(memory_space=pltpu.SMEM)] + [any_space] * 5,
        out_specs=(any_space, any_space),
        scratch_shapes=[
            pltpu.VMEM((ROWS, HEADS * HD), bf16),
            pltpu.VMEM((2, ROWS, HD), bf16),
            pltpu.VMEM((2, ROWS, HD), bf16),
            pltpu.VMEM((HEADS * HD, COLS), bf16),
            pltpu.VMEM((2, HEADS * HD), bf16),
            pltpu.VMEM((2, 2, KVH * HD), bf16),
            pltpu.VMEM((2, HD, HD), bf16),
            pltpu.VMEM((HEADS, ROWS, HD), f32),
            pltpu.VMEM((HEADS, ROWS, HD), f32),
            pltpu.VMEM((HEADS, ROWS, HD), f32),
            pltpu.VMEM((ROWS, HEADS * HD), bf16),
            pltpu.VMEM((HST, 8, HD), bf16),
            pltpu.VMEM((HST * 8, HD), f32),
            pltpu.VMEM((HST, 16, HD), bf16),
            pltpu.VMEM((HST, 16, HD), bf16),
            pltpu.VMEM((HST, 8, HD), bf16),
            pltpu.VMEM((TP, 8, HD), bf16),
            pltpu.VMEM((TP, 8, HD), bf16),
            pltpu.VMEM((TP, 8, HD), bf16),
            pltpu.VMEM((QN, COLS), bf16),
            pltpu.SemaphoreType.DMA((6,)),
            pltpu.SemaphoreType.DMA((HEADS,)),
            pltpu.SemaphoreType.DMA((9,)),
            pltpu.SemaphoreType.DMA((8,)),
        ],
        compiler_params=pltpu.CompilerParams(
            collective_id=0, has_side_effects=True, vmem_limit_bytes=40 * 1024 * 1024
        ),
    )(lengths, ctx_q, ctx_kv, query_q, query_kv, out_weight)


def solution(mesh):
    return jax.shard_map(
        per_device,
        mesh=mesh,
        in_specs=(
            P("hst", "tp"),
            P(None, "hst", None),
            P(),
            P("hst", "tp"),
            P(None, "hst", None),
            P("tp", "hst"),
        ),
        out_specs=(P("hst", "tp"), P(None, "hst")),
        check_vma=False,
    )
```

```python
import jax
import jax.numpy as jnp
from jax import lax
from jax.experimental import pallas as pl
from jax.experimental.pallas import tpu as pltpu
from jax.sharding import PartitionSpec as P

H = 64
KVH = 8
HD = 128
HST = 32
TP = 16
ROWS = 768
HEADS = H // TP
TILE = 256
CHIPS = HST // 2
PIECE = ROWS // CHIPS
QN = 64
COLS = 256
MASKED = -1e30
SCALE2 = HD ** (-0.5) * 1.4426950408889634
MESH = pl.DeviceIdType.MESH


PLANE = sorted(
    [(y, x, c) for y in range(4) for x in range(4) for c in range(2) if y or x or c],
    key=lambda o: -(min(o[0], 4 - o[0]) + min(o[1], 4 - o[1]) + 0.1 * o[2]),
)
ALONG = sorted(range(1, TP), key=lambda o: -min(o, TP - o))


def dot_t(a, b):
    return lax.dot_general(a, b, (((1,), (1,)), ((), ())), preferred_element_type=jnp.float32)


def dot(a, b):
    return jnp.dot(a, b, preferred_element_type=jnp.float32)


def with_ones(values):
    return jnp.concatenate([values, jnp.ones_like(values)], axis=1)


def kernel(
    lengths_hbm,
    ctx_q,
    ctx_kv,
    query_q,
    query_kv,
    out_weight,
    ctx_out,
    query_out,
    lengths,
    cq,
    own,
    anchor,
    weight,
    qq,
    qkv,
    selfkv,
    out1,
    sum1,
    max1,
    gather_q,
    rows_q,
    sent_b,
    got_b,
    att,
    part,
    got_d,
    got_e,
    local_sem,
    send_sem,
    recv_sem,
):
    me = lax.axis_index("hst")
    z = lax.axis_index("tp")
    chip = me // 2
    core = lax.rem(me, 2)
    kv_off = pl.multiple_of((z // 2) * HD, HD)

    py, px = chip // 4, lax.rem(chip, 4)

    def plane_peers():
        for dy, dx, dc in PLANE:
            yield lax.rem(py + dy, 4) * 8 + lax.rem(px + dx, 4) * 2 + lax.rem(core + dc, 2)

    def along_peers():
        for dz in ALONG:
            yield lax.rem(z + dz, TP)

    def at_hst(d):
        return {"hst": d}

    def at_tp(d):
        return {"tp": d}

    load_kv = pltpu.make_async_copy(ctx_kv.at[:, :, pl.ds(kv_off, HD)], own, local_sem.at[0])
    load_cq = pltpu.make_async_copy(ctx_q, cq, local_sem.at[1])
    load_qq = pltpu.make_async_copy(query_q, qq, local_sem.at[2])
    load_qkv = pltpu.make_async_copy(query_kv, qkv, local_sem.at[3])
    load_w = pltpu.make_async_copy(out_weight, weight, local_sem.at[4])
    load_len = pltpu.make_async_copy(lengths_hbm, lengths, local_sem.at[6])
    for copy in (load_len, load_qq, load_kv, load_cq, load_qkv, load_w):
        copy.start()

    barrier = pltpu.get_barrier_semaphore()

    for d in plane_peers():
        pl.semaphore_signal(barrier, inc=1, device_id=at_hst(d), device_id_type=MESH)
    for d in along_peers():
        pl.semaphore_signal(barrier, inc=1, device_id=at_tp(d), device_id_type=MESH)

    load_len.wait()
    own_len = lengths[me]

    diag_row = lax.broadcasted_iota(jnp.int32, (TILE, TILE), 0)
    diag_col = lax.broadcasted_iota(jnp.int32, (TILE, TILE), 1)

    def own_head(h):
        for rb in range(ROWS // TILE):
            rows = pl.ds(rb * TILE, TILE)
            q = cq[rows, h * HD : (h + 1) * HD]
            keys = (rb + 1) * TILE
            s = dot_t(q, own[0, 0:keys, :])
            last = jnp.where(diag_col <= diag_row, s[:, keys - TILE :], MASKED)
            s = last if rb == 0 else jnp.concatenate([s[:, : keys - TILE], last], axis=1)
            m = jnp.max(s, axis=1, keepdims=True) * SCALE2
            p = jnp.exp2(s * SCALE2 - m).astype(jnp.bfloat16)
            o = dot(p, with_ones(own[1, 0:keys, :]))
            out1[h, rows, :] = o[:, :HD]
            sum1[h, rows, :] = o[:, HD:]
            max1[h, rows, :] = jnp.broadcast_to(m, (TILE, HD))

    def live(rb, value):
        rid = rb * TILE + lax.broadcasted_iota(jnp.int32, (TILE, HD), 0)
        return jnp.where(rid < own_len, value, 0.0).astype(jnp.bfloat16)

    def anchor_head(h):
        for rb in range(ROWS // TILE):
            rows = pl.ds(rb * TILE, TILE)
            q = cq[rows, h * HD : (h + 1) * HD]
            s = dot_t(q, anchor[0])
            before = max1[h, rows, :]
            m = jnp.maximum(jnp.max(s, axis=1, keepdims=True) * SCALE2, before[:, :1])
            p = jnp.exp2(s * SCALE2 - m).astype(jnp.bfloat16)
            o = dot(p, with_ones(anchor[1]))
            keep = jnp.exp2(before - m)
            num = out1[h, rows, :] * keep + o[:, :HD]
            den = sum1[h, rows, :] * keep + o[:, HD:]
            ctx_out[rows, h * HD : (h + 1) * HD] = live(rb, num / den)

    def first_head(h):
        for rb in range(ROWS // TILE):
            rows = pl.ds(rb * TILE, TILE)
            ctx_out[rows, h * HD : (h + 1) * HD] = live(rb, out1[h, rows, :] / sum1[h, rows, :])

    def finish_head(h):
        @pl.when(me > 0)
        def _():
            anchor_head(h)

        @pl.when(me == 0)
        def _():
            first_head(h)

    load_qq.wait()
    mine = qq[...].astype(jnp.float32)
    gather_q[pl.ds(me, 1)] = jnp.concatenate(
        [mine[t : t + 1, h * HD : (h + 1) * HD] for t in range(2) for h in range(HEADS)], axis=0
    ).astype(jnp.bfloat16)[None]

    pl.semaphore_wait(barrier, HST - 1 + TP - 1)

    for d in plane_peers():
        pltpu.make_async_remote_copy(
            gather_q.at[me], gather_q.at[me], send_sem.at[0], recv_sem.at[0],
            device_id=at_hst(d), device_id_type=MESH,
        ).start()

    def piece(ref, plane, c):
        return ref.at[plane, pl.ds(pl.multiple_of(c * PIECE, 16), PIECE), :]

    load_kv.wait()

    @pl.when(me == 0)
    def _():
        @pl.loop(1, CHIPS)
        def _(c):
            pltpu.make_async_remote_copy(
                piece(own, 0, c), piece(anchor, 0, c), send_sem.at[1], recv_sem.at[1],
                device_id=at_hst(c * 2), device_id_type=MESH,
            ).start()
            pltpu.make_async_remote_copy(
                piece(own, 1, c), piece(anchor, 1, c), send_sem.at[2], recv_sem.at[1],
                device_id=at_hst(c * 2 + 1), device_id_type=MESH,
            ).start()

        pltpu.make_async_remote_copy(
            piece(own, 1, 0), piece(anchor, 1, 0), send_sem.at[2], recv_sem.at[1],
            device_id=at_hst(1), device_id_type=MESH,
        ).start()

        @pl.loop(1, CHIPS)
        def _(c):
            pltpu.make_async_remote_copy(
                piece(own, 0, 0), piece(anchor, 0, 0), send_sem.at[3], recv_sem.at[2],
                device_id=at_hst(c * 2), device_id_type=MESH,
            ).start()

        pltpu.make_async_remote_copy(
            own.at[0], anchor.at[0], send_sem.at[4], recv_sem.at[3],
            device_id=at_hst(1), device_id_type=MESH,
        ).start()

    load_cq.wait()
    for h in range(HEADS):
        own_head(h)

    pltpu.make_async_copy(
        gather_q.at[pl.ds(0, HST - 1)], gather_q.at[pl.ds(0, HST - 1)], recv_sem.at[0]
    ).wait()
    rows_q[...] = gather_q[...].astype(jnp.float32).reshape(HST * 8, HD)
    q_all = jnp.concatenate(
        [rows_q[pl.ds(h, QN, stride=HEADS), :] for h in range(HEADS)], axis=0
    ).astype(jnp.bfloat16)
    load_qkv.wait()
    for plane in range(2):
        tiny = qkv[plane, :, pl.ds(kv_off, HD)].astype(jnp.float32)
        selfkv[plane] = jnp.concatenate(
            [tiny, jnp.zeros((HD - 2, HD), jnp.float32)], axis=0
        ).astype(jnp.bfloat16)
    s_ctx = dot_t(q_all, own[0])
    s_ctx = jnp.where(
        lax.broadcasted_iota(jnp.int32, s_ctx.shape, 1) < own_len, s_ctx, MASKED
    )
    s_self = dot_t(q_all, selfkv[0])
    token = lax.rem(lax.broadcasted_iota(jnp.int32, s_self.shape, 0), QN)
    key = lax.broadcasted_iota(jnp.int32, s_self.shape, 1)
    s_self = jnp.where((key < 2) & (me * 2 + key <= token), s_self, MASKED)
    peak = jnp.maximum(
        jnp.max(s_ctx, axis=1, keepdims=True), jnp.max(s_self, axis=1, keepdims=True)
    )
    peak = (peak * SCALE2).astype(jnp.bfloat16).astype(jnp.float32)
    p_ctx = jnp.exp2(s_ctx * SCALE2 - peak).astype(jnp.bfloat16)
    p_self = jnp.exp2(s_self * SCALE2 - peak).astype(jnp.bfloat16)
    o = dot(p_ctx, with_ones(own[1])) + dot(p_self, with_ones(selfkv[1]))
    lane = lax.broadcasted_iota(jnp.int32, (HEADS * QN, HD), 1)
    stats = jnp.where(lane < HD // 2, jnp.broadcast_to(peak, (HEADS * QN, HD)), o[:, HD:])
    sent_b[...] = jnp.concatenate(
        [o[:, :HD].reshape(HST, 8, HD), stats.reshape(HST, 8, HD)], axis=1
    ).astype(jnp.bfloat16)

    for d in plane_peers():
        pltpu.make_async_remote_copy(
            sent_b.at[d], got_b.at[me], send_sem.at[5], recv_sem.at[4],
            device_id=at_hst(d), device_id_type=MESH,
        ).start()

    got_b[pl.ds(me, 1)] = sent_b[pl.ds(me, 1)]

    @pl.when(me > 0)
    def _():
        pltpu.make_async_copy(
            piece(anchor, 0, 0), piece(anchor, 0, 0), recv_sem.at[1]
        ).wait()

        @pl.loop(1, CHIPS)
        def _(k):
            c = lax.rem(chip + k, CHIPS)

            @pl.when(c * 2 + core > 0)
            def _():
                pltpu.make_async_remote_copy(
                    piece(anchor, core, chip), piece(anchor, core, chip),
                    send_sem.at[3], recv_sem.at[2],
                    device_id=at_hst(c * 2 + core), device_id_type=MESH,
                ).start()

    pltpu.make_async_copy(
        got_b.at[pl.ds(0, HST - 1)], got_b.at[pl.ds(0, HST - 1)], recv_sem.at[4]
    ).wait()
    terms = got_b[...].astype(jnp.float32)
    value, stat = terms[:, :8], terms[:, 8:]
    turned = pltpu.roll(stat, HD // 2, 2)
    low = lax.broadcasted_iota(jnp.int32, stat.shape, 2) < HD // 2
    peaks = jnp.where(low, stat, turned)
    sums = jnp.where(low, turned, stat)
    factor = jnp.exp2(peaks - jnp.max(peaks, axis=0, keepdims=True))
    attended = jnp.sum(factor * value, axis=0) / jnp.sum(factor * sums, axis=0)
    att[pl.ds(me, 1)] = attended.astype(jnp.bfloat16)[None]

    for d in plane_peers():
        pltpu.make_async_remote_copy(
            att.at[me], att.at[me], send_sem.at[6], recv_sem.at[5],
            device_id=at_hst(d), device_id_type=MESH,
        ).start()

    @pl.when(me > 0)
    def _():
        pltpu.make_async_copy(
            anchor.at[0, pl.ds(0, ROWS - PIECE)], anchor.at[0, pl.ds(0, ROWS - PIECE)], recv_sem.at[2]
        ).wait()

    @pl.when(me > 1)
    def _():
        pltpu.make_async_remote_copy(
            anchor.at[core], anchor.at[core], send_sem.at[4], recv_sem.at[3],
            device_id=at_hst(me + 1 - 2 * core), device_id_type=MESH,
        ).start()

    load_w.wait()
    pltpu.make_async_copy(
        att.at[pl.ds(0, HST - 1)], att.at[pl.ds(0, HST - 1)], recv_sem.at[5]
    ).wait()
    rows = att[...].astype(jnp.float32).reshape(HEADS, QN, HD)
    wide = jnp.concatenate([rows[h] for h in range(HEADS)], axis=1).astype(jnp.bfloat16)
    partial = dot(wide, weight[...])
    for t in range(TP):
        r, c = t // 2, t % 2
        part[t] = partial[r * 8 : r * 8 + 8, c * HD : (c + 1) * HD].astype(jnp.bfloat16)

    for d in along_peers():
        pltpu.make_async_remote_copy(
            part.at[d], got_d.at[z], send_sem.at[7], recv_sem.at[6],
            device_id=at_tp(d), device_id_type=MESH,
        ).start()

    got_d[pl.ds(z, 1)] = part[pl.ds(z, 1)]
    @pl.when(me > 0)
    def _():
        pltpu.make_async_copy(anchor.at[0], anchor.at[0], recv_sem.at[3]).wait()

    finish_head(0)
    finish_head(1)

    pltpu.make_async_copy(
        got_d.at[pl.ds(0, TP - 1)], got_d.at[pl.ds(0, TP - 1)], recv_sem.at[6]
    ).wait()
    total = jnp.sum(got_d[...].astype(jnp.float32), axis=0)
    got_e[pl.ds(z, 1)] = total.astype(jnp.bfloat16)[None]

    for d in along_peers():
        pltpu.make_async_remote_copy(
            got_e.at[z], got_e.at[z], send_sem.at[8], recv_sem.at[7],
            device_id=at_tp(d), device_id_type=MESH,
        ).start()

    finish_head(2)
    finish_head(3)

    pltpu.make_async_copy(
        got_e.at[pl.ds(0, TP - 1)], got_e.at[pl.ds(0, TP - 1)], recv_sem.at[7]
    ).wait()
    tiles = got_e[...].astype(jnp.float32)
    query_out[...] = jnp.concatenate(
        [
            jnp.concatenate([tiles[2 * r], tiles[2 * r + 1]], axis=1)
            for r in range(TP // 2)
        ],
        axis=0,
    ).astype(jnp.bfloat16)

    for sem, ref in (
        (0, gather_q.at[pl.ds(0, HST - 1)]),
        (5, got_b.at[pl.ds(0, HST - 1)]),
        (6, att.at[pl.ds(0, HST - 1)]),
        (7, got_d.at[pl.ds(0, TP - 1)]),
        (8, got_e.at[pl.ds(0, TP - 1)]),
    ):
        pltpu.make_async_copy(ref, ref, send_sem.at[sem]).wait()

    def sent(sem, rows):
        ref = own.at[0, pl.ds(0, rows)]
        pltpu.make_async_copy(ref, ref, send_sem.at[sem]).wait()

    @pl.when(me == 0)
    def _():
        sent(1, ROWS - PIECE)
        sent(2, ROWS)

    @pl.when(core + (me == 0) > 0)
    def _():
        sent(3, ROWS - PIECE)

    @pl.when(core + (me == 0) == 0)
    def _():
        sent(3, ROWS - 2 * PIECE)

    @pl.when((me == 0) | (me > 1))
    def _():
        sent(4, ROWS)


def per_device(ctx_q, ctx_kv, lengths, query_q, query_kv, out_weight):
    bf16, f32 = jnp.bfloat16, jnp.float32
    hbm = pl.BlockSpec(memory_space=pltpu.HBM)
    vmem = pl.BlockSpec(memory_space=pltpu.VMEM)
    return pl.pallas_call(
        kernel,
        out_shape=(
            pltpu.VMEM((ROWS, HEADS * HD), bf16),
            pltpu.VMEM((QN, COLS), bf16),
        ),
        in_specs=[hbm] * 6,
        out_specs=(vmem, vmem),
        scratch_shapes=[
            pltpu.SMEM((HST,), jnp.int32),
            pltpu.VMEM((ROWS, HEADS * HD), bf16),
            pltpu.VMEM((2, ROWS, HD), bf16),
            pltpu.VMEM((2, ROWS, HD), bf16),
            pltpu.VMEM((HEADS * HD, COLS), bf16),
            pltpu.VMEM((2, HEADS * HD), bf16),
            pltpu.VMEM((2, 2, KVH * HD), bf16),
            pltpu.VMEM((2, HD, HD), bf16),
            pltpu.VMEM((HEADS, ROWS, HD), f32),
            pltpu.VMEM((HEADS, ROWS, HD), f32),
            pltpu.VMEM((HEADS, ROWS, HD), f32),
            pltpu.VMEM((HST, 8, HD), bf16),
            pltpu.VMEM((HST * 8, HD), f32),
            pltpu.VMEM((HST, 16, HD), bf16),
            pltpu.VMEM((HST, 16, HD), bf16),
            pltpu.VMEM((HST, 8, HD), bf16),
            pltpu.VMEM((TP, 8, HD), bf16),
            pltpu.VMEM((TP, 8, HD), bf16),
            pltpu.VMEM((TP, 8, HD), bf16),
            pltpu.SemaphoreType.DMA((7,)),
            pltpu.SemaphoreType.DMA((9,)),
            pltpu.SemaphoreType.DMA((8,)),
        ],
        compiler_params=pltpu.CompilerParams(
            collective_id=0, has_side_effects=True, vmem_limit_bytes=48 * 1024 * 1024
        ),
    )(*(pltpu.with_memory_space_constraint(a, pltpu.HBM) for a in (lengths, ctx_q, ctx_kv, query_q, query_kv, out_weight)))


def solution(mesh):
    return jax.shard_map(
        per_device,
        mesh=mesh,
        in_specs=(
            P("hst", "tp"),
            P(None, "hst", None),
            P(),
            P("hst", "tp"),
            P(None, "hst", None),
            P("tp", "hst"),
        ),
        out_specs=(P("hst", "tp"), P(None, "hst")),
        check_vma=False,
    )
```

```python
import jax
import jax.numpy as jnp
from jax import lax
from jax.experimental import pallas as pl
from jax.experimental.pallas import tpu as pltpu
from jax.sharding import PartitionSpec as P

H = 64
KVH = 8
HD = 128
HST = 32
TP = 16
ROWS = 768
HEADS = H // TP
TILE = 256
CHIPS = HST // 2
PIECE = ROWS // CHIPS
QN = 64
COLS = 256
MASKED = -1e30
SCALE2 = HD ** (-0.5) * 1.4426950408889634
MESH = pl.DeviceIdType.MESH


CHIP_OFFSETS = sorted(
    [(y, x) for y in range(4) for x in range(4) if y or x],
    key=lambda o: -(min(o[0], 4 - o[0]) + min(o[1], 4 - o[1])),
)
TILES = 8
FIRST = 11


def dot_t(a, b):
    return lax.dot_general(a, b, (((1,), (1,)), ((), ())), preferred_element_type=jnp.float32)


def dot(a, b):
    return jnp.dot(a, b, preferred_element_type=jnp.float32)


def with_ones(values):
    return jnp.concatenate([values, jnp.ones_like(values)], axis=1)


def kernel(
    lengths_hbm,
    ctx_q,
    ctx_kv,
    query_q,
    query_kv,
    out_weight,
    ctx_out,
    query_out,
    lengths,
    cq,
    own,
    anchor,
    weight,
    qq,
    qkv,
    selfkv,
    out1,
    sum1,
    max1,
    gather_q,
    rows_q,
    sent_b,
    got_b,
    att,
    part,
    got_d,
    summed,
    got_e,
    local_sem,
    send_sem,
    recv_sem,
    ready,
):
    me = lax.axis_index("hst")
    z = lax.axis_index("tp")
    chip = me // 2
    core = lax.rem(me, 2)
    kv_off = pl.multiple_of((z // 2) * HD, HD)

    py, px = chip // 4, lax.rem(chip, 4)

    mate = me + 1 - 2 * core
    column = chip * 2 + 1
    tile = lax.rem(z + TP - FIRST, TP)
    adds = (core == 1) & (tile < TILES)

    def other_chips():
        for dy, dx in CHIP_OFFSETS:
            yield lax.rem(py + dy, 4) * 4 + lax.rem(px + dx, 4)

    def at_hst(d):
        return {"hst": d}

    load_kv = pltpu.make_async_copy(ctx_kv.at[:, :, pl.ds(kv_off, HD)], own, local_sem.at[0])
    load_cq = pltpu.make_async_copy(ctx_q, cq, local_sem.at[1])
    load_qq = pltpu.make_async_copy(query_q, qq, local_sem.at[2])
    load_qkv = pltpu.make_async_copy(query_kv, qkv, local_sem.at[3])
    load_w = pltpu.make_async_copy(out_weight, weight, local_sem.at[4])
    load_len = pltpu.make_async_copy(lengths_hbm, lengths, local_sem.at[6])
    for copy in (load_len, load_qq, load_kv, load_cq, load_qkv, load_w):
        copy.start()

    barrier = pltpu.get_barrier_semaphore()

    def greet(**where):
        pl.semaphore_signal(barrier, inc=1, device_id=where, device_id_type=MESH)

    for c in other_chips():
        greet(hst=c * 2)
    for dz in (8, 7, 9, 6, 10, 5, 11, 4, 12, 3, 13, 2, 14, 1, 15):
        greet(hst=column, tp=lax.rem(z + dz, TP))
    greet(hst=mate)

    load_len.wait()
    own_len = lengths[me]

    diag_row = lax.broadcasted_iota(jnp.int32, (TILE, TILE), 0)
    diag_col = lax.broadcasted_iota(jnp.int32, (TILE, TILE), 1)

    def own_head(h):
        for rb in range(ROWS // TILE):
            rows = pl.ds(rb * TILE, TILE)
            q = cq[rows, h * HD : (h + 1) * HD]
            keys = (rb + 1) * TILE
            s = dot_t(q, own[0, 0:keys, :])
            last = jnp.where(diag_col <= diag_row, s[:, keys - TILE :], MASKED)
            s = last if rb == 0 else jnp.concatenate([s[:, : keys - TILE], last], axis=1)
            m = jnp.max(s, axis=1, keepdims=True) * SCALE2
            p = jnp.exp2(s * SCALE2 - m).astype(jnp.bfloat16)
            o = dot(p, with_ones(own[1, 0:keys, :]))
            out1[h, rows, :] = o[:, :HD]
            sum1[h, rows, :] = o[:, HD:]
            max1[h, rows, :] = jnp.broadcast_to(m, (TILE, HD))

    def live(rb, value):
        rid = rb * TILE + lax.broadcasted_iota(jnp.int32, (TILE, HD), 0)
        return jnp.where(rid < own_len, value, 0.0).astype(jnp.bfloat16)

    def anchor_head(h):
        for rb in range(ROWS // TILE):
            rows = pl.ds(rb * TILE, TILE)
            q = cq[rows, h * HD : (h + 1) * HD]
            s = dot_t(q, anchor[0])
            before = max1[h, rows, :]
            m = jnp.maximum(jnp.max(s, axis=1, keepdims=True) * SCALE2, before[:, :1])
            p = jnp.exp2(s * SCALE2 - m).astype(jnp.bfloat16)
            o = dot(p, with_ones(anchor[1]))
            keep = jnp.exp2(before - m)
            num = out1[h, rows, :] * keep + o[:, :HD]
            den = sum1[h, rows, :] * keep + o[:, HD:]
            ctx_out[rows, h * HD : (h + 1) * HD] = live(rb, num / den)

    def first_head(h):
        for rb in range(ROWS // TILE):
            rows = pl.ds(rb * TILE, TILE)
            ctx_out[rows, h * HD : (h + 1) * HD] = live(rb, out1[h, rows, :] / sum1[h, rows, :])

    def finish_head(h):
        @pl.when(me > 0)
        def _():
            anchor_head(h)

        @pl.when(me == 0)
        def _():
            first_head(h)

    load_qq.wait()
    mine = qq[...].astype(jnp.float32)
    gather_q[pl.ds(me, 1)] = jnp.concatenate(
        [mine[t : t + 1, h * HD : (h + 1) * HD] for t in range(2) for h in range(HEADS)], axis=0
    ).astype(jnp.bfloat16)[None]

    @pl.when(core == 0)
    def _():
        pl.semaphore_wait(barrier, HST - 1)
        pl.semaphore_signal(ready.at[0], inc=1, device_id=at_hst(mate), device_id_type=MESH)

    @pl.when(core == 1)
    def _():
        pl.semaphore_wait(ready.at[0], 1)

    def send_a(d):
        pltpu.make_async_remote_copy(
            gather_q.at[me], gather_q.at[me], send_sem.at[0], recv_sem.at[0],
            device_id=at_hst(d), device_id_type=MESH,
        ).start()

    for c in other_chips():
        send_a(c * 2)
        send_a(c * 2 + 1)
    send_a(mate)

    def piece(ref, plane, c):
        return ref.at[plane, pl.ds(pl.multiple_of(c * PIECE, 16), PIECE), :]

    load_kv.wait()

    @pl.when(me == 0)
    def _():
        @pl.loop(1, CHIPS)
        def _(c):
            pltpu.make_async_remote_copy(
                piece(own, 0, c), piece(anchor, 0, c), send_sem.at[1], recv_sem.at[1],
                device_id=at_hst(c * 2), device_id_type=MESH,
            ).start()
            pltpu.make_async_remote_copy(
                piece(own, 1, c), piece(anchor, 1, c), send_sem.at[2], recv_sem.at[1],
                device_id=at_hst(c * 2 + 1), device_id_type=MESH,
            ).start()

        pltpu.make_async_remote_copy(
            piece(own, 1, 0), piece(anchor, 1, 0), send_sem.at[2], recv_sem.at[1],
            device_id=at_hst(1), device_id_type=MESH,
        ).start()

        @pl.loop(1, CHIPS)
        def _(c):
            pltpu.make_async_remote_copy(
                piece(own, 0, 0), piece(anchor, 0, 0), send_sem.at[3], recv_sem.at[2],
                device_id=at_hst(c * 2), device_id_type=MESH,
            ).start()

        pltpu.make_async_remote_copy(
            own.at[0], anchor.at[0], send_sem.at[4], recv_sem.at[3],
            device_id=at_hst(1), device_id_type=MESH,
        ).start()

    load_cq.wait()
    for h in range(HEADS):
        own_head(h)

    pltpu.make_async_copy(
        gather_q.at[pl.ds(0, HST - 1)], gather_q.at[pl.ds(0, HST - 1)], recv_sem.at[0]
    ).wait()
    rows_q[...] = gather_q[...].astype(jnp.float32).reshape(HST * 8, HD)
    q_all = jnp.concatenate(
        [rows_q[pl.ds(h, QN, stride=HEADS), :] for h in range(HEADS)], axis=0
    ).astype(jnp.bfloat16)
    load_qkv.wait()
    for plane in range(2):
        tiny = qkv[plane, :, pl.ds(kv_off, HD)].astype(jnp.float32)
        selfkv[plane] = jnp.concatenate(
            [tiny, jnp.zeros((HD - 2, HD), jnp.float32)], axis=0
        ).astype(jnp.bfloat16)
    s_ctx = dot_t(q_all, own[0])
    s_ctx = jnp.where(
        lax.broadcasted_iota(jnp.int32, s_ctx.shape, 1) < own_len, s_ctx, MASKED
    )
    s_self = dot_t(q_all, selfkv[0])
    token = lax.rem(lax.broadcasted_iota(jnp.int32, s_self.shape, 0), QN)
    key = lax.broadcasted_iota(jnp.int32, s_self.shape, 1)
    s_self = jnp.where((key < 2) & (me * 2 + key <= token), s_self, MASKED)
    peak = jnp.maximum(
        jnp.max(s_ctx, axis=1, keepdims=True), jnp.max(s_self, axis=1, keepdims=True)
    )
    peak = (peak * SCALE2).astype(jnp.bfloat16).astype(jnp.float32)
    p_ctx = jnp.exp2(s_ctx * SCALE2 - peak).astype(jnp.bfloat16)
    p_self = jnp.exp2(s_self * SCALE2 - peak).astype(jnp.bfloat16)
    o = dot(p_ctx, with_ones(own[1])) + dot(p_self, with_ones(selfkv[1]))
    lane = lax.broadcasted_iota(jnp.int32, (HEADS * QN, HD), 1)
    stats = jnp.where(lane < HD // 2, jnp.broadcast_to(peak, (HEADS * QN, HD)), o[:, HD:])
    sent_b[...] = jnp.concatenate(
        [o[:, :HD].reshape(CHIPS, 16, HD), stats.reshape(CHIPS, 16, HD)], axis=1
    ).astype(jnp.bfloat16)

    def send_b(c):
        pltpu.make_async_remote_copy(
            sent_b.at[c], got_b.at[me], send_sem.at[5], recv_sem.at[4],
            device_id=at_hst(c * 2 + 1), device_id_type=MESH,
        ).start()

    for c in other_chips():
        send_b(c)

    @pl.when(core == 0)
    def _():
        send_b(chip)

    @pl.when(core == 1)
    def _():
        got_b[pl.ds(me, 1)] = sent_b[pl.ds(chip, 1)]

    @pl.when(me > 0)
    def _():
        pltpu.make_async_copy(
            piece(anchor, 0, 0), piece(anchor, 0, 0), recv_sem.at[1]
        ).wait()

        @pl.loop(1, CHIPS)
        def _(k):
            c = lax.rem(chip + k, CHIPS)

            @pl.when(c * 2 + core > 0)
            def _():
                pltpu.make_async_remote_copy(
                    piece(anchor, core, chip), piece(anchor, core, chip),
                    send_sem.at[3], recv_sem.at[2],
                    device_id=at_hst(c * 2 + core), device_id_type=MESH,
                ).start()

    def send_c(d):
        pltpu.make_async_remote_copy(
            att.at[chip], att.at[chip], send_sem.at[6], recv_sem.at[5],
            device_id=at_hst(d), device_id_type=MESH,
        ).start()

    @pl.when(core == 1)
    def _():
        pltpu.make_async_copy(
            got_b.at[pl.ds(0, HST - 1)], got_b.at[pl.ds(0, HST - 1)], recv_sem.at[4]
        ).wait()
        terms = got_b[...].astype(jnp.float32)
        value, stat = terms[:, :16], terms[:, 16:]
        turned = pltpu.roll(stat, HD // 2, 2)
        low = lax.broadcasted_iota(jnp.int32, stat.shape, 2) < HD // 2
        peaks = jnp.where(low, stat, turned)
        sums = jnp.where(low, turned, stat)
        factor = jnp.exp2(peaks - jnp.max(peaks, axis=0, keepdims=True))
        attended = jnp.sum(factor * value, axis=0) / jnp.sum(factor * sums, axis=0)
        att[pl.ds(chip, 1)] = attended.astype(jnp.bfloat16)[None]

        for c in other_chips():
            send_c(c * 2)
            send_c(c * 2 + 1)
        send_c(mate)

    @pl.when(me > 0)
    def _():
        pltpu.make_async_copy(
            anchor.at[0, pl.ds(0, ROWS - PIECE)], anchor.at[0, pl.ds(0, ROWS - PIECE)], recv_sem.at[2]
        ).wait()

    @pl.when(me > 1)
    def _():
        pltpu.make_async_remote_copy(
            anchor.at[core], anchor.at[core], send_sem.at[4], recv_sem.at[3],
            device_id=at_hst(mate), device_id_type=MESH,
        ).start()

    load_w.wait()

    def landed(ref, n, sem):
        pltpu.make_async_copy(ref.at[pl.ds(0, n)], ref.at[pl.ds(0, n)], sem).wait()

    @pl.when(core == 0)
    def _():
        landed(att, CHIPS, recv_sem.at[5])

    @pl.when(core == 1)
    def _():
        landed(att, CHIPS - 1, recv_sem.at[5])

    rows = att[...].astype(jnp.float32).reshape(HEADS, QN, HD)
    wide = jnp.concatenate([rows[h] for h in range(HEADS)], axis=1).astype(jnp.bfloat16)
    partial = dot(wide, weight[...]).astype(jnp.bfloat16)
    for t in range(TILES):
        r, c = t // 2, t % 2
        part[t] = partial[r * 16 : r * 16 + 16, c * HD : (c + 1) * HD]

    @pl.when(core == 1)
    def _():
        pl.semaphore_wait(barrier, 2 * TP - 1)
        pl.semaphore_signal(ready.at[1], inc=1, device_id=at_hst(mate), device_id_type=MESH)

    @pl.when(core == 0)
    def _():
        pl.semaphore_wait(ready.at[1], 1)

    slot = core * TP + z
    for t in (7, 6, 0, 5, 4, 3, 2, 1):
        r = (FIRST + t) % TP

        @pl.when((core == 0) | (z != r))
        def _():
            pltpu.make_async_remote_copy(
                part.at[t], got_d.at[slot], send_sem.at[7], recv_sem.at[6],
                device_id={"hst": column, "tp": r}, device_id_type=MESH,
            ).start()

        @pl.when((core == 1) & (z == r))
        def _():
            got_d[pl.ds(slot, 1)] = part[pl.ds(t, 1)]

    @pl.when(me > 0)
    def _():
        pltpu.make_async_copy(anchor.at[0], anchor.at[0], recv_sem.at[3]).wait()

    finish_head(0)
    finish_head(1)

    def send_e(src, where):
        pltpu.make_async_remote_copy(
            src, got_e.at[tile], send_sem.at[8], recv_sem.at[7],
            device_id=where, device_id_type=MESH,
        ).start()

    @pl.when(adds)
    def _():
        landed(got_d, 2 * TP - 1, recv_sem.at[6])
        total = got_d[...].astype(jnp.float32)
        summed[...] = jnp.sum(total[:TP], axis=0).astype(jnp.bfloat16)
        got_e[pl.ds(tile, 1)] = jnp.sum(total[TP:], axis=0).astype(jnp.bfloat16)[None]
        for d in range(TP):
            send_e(summed, {"hst": column - 1, "tp": d})

            @pl.when(z != d)
            def _():
                send_e(got_e.at[tile], {"hst": column, "tp": d})

    finish_head(2)
    finish_head(3)

    @pl.when(adds)
    def _():
        landed(got_e, TILES - 1, recv_sem.at[7])

    @pl.when(jnp.logical_not(adds))
    def _():
        landed(got_e, TILES, recv_sem.at[7])

    for t in range(TILES):
        query_out[t // 2 * 16 : t // 2 * 16 + 16, t % 2 * HD : (t % 2 + 1) * HD] = got_e[t]

    landed(gather_q, HST - 1, send_sem.at[0])

    @pl.when(core == 0)
    def _():
        landed(sent_b, CHIPS, send_sem.at[5])
        landed(part, TILES, send_sem.at[7])

    @pl.when(core == 1)
    def _():
        landed(sent_b, CHIPS - 1, send_sem.at[5])
        landed(got_d, 2 * CHIPS - 1, send_sem.at[6])

    @pl.when(adds)
    def _():
        landed(part, TILES - 1, send_sem.at[7])
        landed(got_d, 2 * TP - 1, send_sem.at[8])

    @pl.when((core == 1) & (tile >= TILES))
    def _():
        landed(part, TILES, send_sem.at[7])

    def sent(sem, rows):
        ref = own.at[0, pl.ds(0, rows)]
        pltpu.make_async_copy(ref, ref, send_sem.at[sem]).wait()

    @pl.when(me == 0)
    def _():
        sent(1, ROWS - PIECE)
        sent(2, ROWS)

    @pl.when(core + (me == 0) > 0)
    def _():
        sent(3, ROWS - PIECE)

    @pl.when(core + (me == 0) == 0)
    def _():
        sent(3, ROWS - 2 * PIECE)

    @pl.when((me == 0) | (me > 1))
    def _():
        sent(4, ROWS)


def per_device(ctx_q, ctx_kv, lengths, query_q, query_kv, out_weight):
    bf16, f32 = jnp.bfloat16, jnp.float32
    hbm = pl.BlockSpec(memory_space=pltpu.HBM)
    vmem = pl.BlockSpec(memory_space=pltpu.VMEM)
    return pl.pallas_call(
        kernel,
        out_shape=(
            pltpu.VMEM((ROWS, HEADS * HD), bf16),
            pltpu.VMEM((QN, COLS), bf16),
        ),
        in_specs=[hbm] * 6,
        out_specs=(vmem, vmem),
        scratch_shapes=[
            pltpu.SMEM((HST,), jnp.int32),
            pltpu.VMEM((ROWS, HEADS * HD), bf16),
            pltpu.VMEM((2, ROWS, HD), bf16),
            pltpu.VMEM((2, ROWS, HD), bf16),
            pltpu.VMEM((HEADS * HD, COLS), bf16),
            pltpu.VMEM((2, HEADS * HD), bf16),
            pltpu.VMEM((2, 2, KVH * HD), bf16),
            pltpu.VMEM((2, HD, HD), bf16),
            pltpu.VMEM((HEADS, ROWS, HD), f32),
            pltpu.VMEM((HEADS, ROWS, HD), f32),
            pltpu.VMEM((HEADS, ROWS, HD), f32),
            pltpu.VMEM((HST, 8, HD), bf16),
            pltpu.VMEM((HST * 8, HD), f32),
            pltpu.VMEM((CHIPS, 32, HD), bf16),
            pltpu.VMEM((HST, 32, HD), bf16),
            pltpu.VMEM((CHIPS, 16, HD), bf16),
            pltpu.VMEM((TILES, 16, HD), bf16),
            pltpu.VMEM((2 * TP, 16, HD), bf16),
            pltpu.VMEM((16, HD), bf16),
            pltpu.VMEM((TILES, 16, HD), bf16),
            pltpu.SemaphoreType.DMA((7,)),
            pltpu.SemaphoreType.DMA((9,)),
            pltpu.SemaphoreType.DMA((8,)),
            pltpu.SemaphoreType.REGULAR((2,)),
        ],
        compiler_params=pltpu.CompilerParams(
            collective_id=0, has_side_effects=True, vmem_limit_bytes=48 * 1024 * 1024
        ),
    )(*(pltpu.with_memory_space_constraint(a, pltpu.HBM) for a in (lengths, ctx_q, ctx_kv, query_q, query_kv, out_weight)))


def solution(mesh):
    return jax.shard_map(
        per_device,
        mesh=mesh,
        in_specs=(
            P("hst", "tp"),
            P(None, "hst", None),
            P(),
            P("hst", "tp"),
            P(None, "hst", None),
            P("tp", "hst"),
        ),
        out_specs=(P("hst", "tp"), P(None, "hst")),
        check_vma=False,
    )
```

```python
import jax
import jax.numpy as jnp
from jax import lax
from jax.experimental import pallas as pl
from jax.experimental.pallas import tpu as pltpu
from jax.sharding import PartitionSpec as P

H = 64
KVH = 8
HD = 128
HST = 32
TP = 16
ROWS = 768
HEADS = H // TP
TILE = 256
CHIPS = HST // 2
PIECE = ROWS // CHIPS
QN = 64
COLS = 256
MASKED = -1e30
SCALE2 = HD ** (-0.5) * 1.4426950408889634
MESH = pl.DeviceIdType.MESH


CHIP_OFFSETS = sorted(
    [(y, x) for y in range(4) for x in range(4) if y or x],
    key=lambda o: -(min(o[0], 4 - o[0]) + min(o[1], 4 - o[1])),
)
TILES = 8
FIRST = 10


def dot_t(a, b):
    return lax.dot_general(a, b, (((1,), (1,)), ((), ())), preferred_element_type=jnp.float32)


def dot(a, b):
    return jnp.dot(a, b, preferred_element_type=jnp.float32)


def with_ones(values):
    return jnp.concatenate([values, jnp.ones_like(values)], axis=1)


def kernel(
    lengths_hbm,
    ctx_q,
    ctx_kv,
    query_q,
    query_kv,
    out_weight,
    ctx_out,
    query_out,
    lengths,
    cq,
    own,
    anchor,
    values_piece,
    weight,
    qq,
    qkv,
    selfkv,
    out1,
    sum1,
    max1,
    gather_q,
    handed_q,
    rows_q,
    sent_b,
    got_b,
    att,
    part,
    got_d,
    summed,
    got_e,
    local_sem,
    send_sem,
    recv_sem,
    ready,
):
    me = lax.axis_index("hst")
    z = lax.axis_index("tp")
    chip = me // 2
    core = lax.rem(me, 2)
    kv_off = pl.multiple_of((z // 2) * HD, HD)

    py, px = chip // 4, lax.rem(chip, 4)

    mate = me + 1 - 2 * core
    column = chip * 2 + 1
    tile = lax.rem(z + TP - FIRST, TP)
    adds = (core == 1) & (tile < TILES)

    def other_chips():
        for dy, dx in CHIP_OFFSETS:
            yield lax.rem(py + dy, 4) * 4 + lax.rem(px + dx, 4)

    def at_hst(d):
        return {"hst": d}

    load_kv = pltpu.make_async_copy(ctx_kv.at[:, :, pl.ds(kv_off, HD)], own, local_sem.at[0])
    load_cq = pltpu.make_async_copy(ctx_q, cq, local_sem.at[1])
    load_qq = pltpu.make_async_copy(query_q, qq, local_sem.at[2])
    load_qkv = pltpu.make_async_copy(query_kv, qkv, local_sem.at[3])
    load_w = pltpu.make_async_copy(out_weight, weight, local_sem.at[4])
    load_len = pltpu.make_async_copy(lengths_hbm, lengths, local_sem.at[6])
    load_qq.start()

    barrier = pltpu.get_barrier_semaphore()

    def greet(**where):
        pl.semaphore_signal(barrier, inc=1, device_id=where, device_id_type=MESH)

    @pl.when(core == 0)
    def _():
        for c in other_chips():
            greet(hst=c * 2)

    greet(hst=mate)
    for copy in (load_kv, load_cq, load_len, load_qkv, load_w):
        copy.start()
    for dz in (8, 7, 9, 6, 10, 5, 11, 4, 12, 3, 13, 2, 14, 1, 15):
        greet(hst=column, tp=lax.rem(z + dz, TP))

    diag_row = lax.broadcasted_iota(jnp.int32, (TILE, TILE), 0)
    diag_col = lax.broadcasted_iota(jnp.int32, (TILE, TILE), 1)

    def own_head(h):
        for rb in range(ROWS // TILE):
            rows = pl.ds(rb * TILE, TILE)
            q = cq[rows, h * HD : (h + 1) * HD]
            keys = (rb + 1) * TILE
            s = dot_t(q, own[0, 0:keys, :])
            last = jnp.where(diag_col <= diag_row, s[:, keys - TILE :], MASKED)
            s = last if rb == 0 else jnp.concatenate([s[:, : keys - TILE], last], axis=1)
            m = jnp.max(s, axis=1, keepdims=True) * SCALE2
            p = jnp.exp2(s * SCALE2 - m).astype(jnp.bfloat16)
            o = dot(p, with_ones(own[1, 0:keys, :]))
            out1[h, rows, :] = o[:, :HD]
            sum1[h, rows, :] = o[:, HD:]
            max1[h, rows, :] = jnp.broadcast_to(m, (TILE, HD))

    def live(rb, value):
        own_len = lengths[me]
        rid = rb * TILE + lax.broadcasted_iota(jnp.int32, (TILE, HD), 0)
        return jnp.where(rid < own_len, value, 0.0).astype(jnp.bfloat16)

    def anchor_head(h):
        for rb in range(ROWS // TILE):
            rows = pl.ds(rb * TILE, TILE)
            q = cq[rows, h * HD : (h + 1) * HD]
            s = dot_t(q, anchor[0])
            before = max1[h, rows, :]
            m = jnp.maximum(jnp.max(s, axis=1, keepdims=True) * SCALE2, before[:, :1])
            p = jnp.exp2(s * SCALE2 - m).astype(jnp.bfloat16)
            o = dot(p, with_ones(anchor[1]))
            keep = jnp.exp2(before - m)
            num = out1[h, rows, :] * keep + o[:, :HD]
            den = sum1[h, rows, :] * keep + o[:, HD:]
            ctx_out[rows, h * HD : (h + 1) * HD] = live(rb, num / den)

    def first_head(h):
        for rb in range(ROWS // TILE):
            rows = pl.ds(rb * TILE, TILE)
            ctx_out[rows, h * HD : (h + 1) * HD] = live(rb, out1[h, rows, :] / sum1[h, rows, :])

    def finish_head(h):
        @pl.when(me > 0)
        def _():
            anchor_head(h)

        @pl.when(me == 0)
        def _():
            first_head(h)

    load_qq.wait()
    mine = qq[...].astype(jnp.float32)
    gather_q[pl.ds(me, 1)] = jnp.concatenate(
        [mine[t : t + 1, h * HD : (h + 1) * HD] for t in range(2) for h in range(HEADS)], axis=0
    ).astype(jnp.bfloat16)[None]

    @pl.when(core == 0)
    def _():
        pl.semaphore_wait(barrier, CHIPS)
        pl.semaphore_signal(ready.at[0], inc=1, device_id=at_hst(mate), device_id_type=MESH)

    @pl.when(core == 1)
    def _():
        pl.semaphore_wait(ready.at[0], 1)

    def send_a(d):
        pltpu.make_async_remote_copy(
            gather_q.at[me], gather_q.at[me], send_sem.at[0], recv_sem.at[0],
            device_id=at_hst(d), device_id_type=MESH,
        ).start()

    for c in other_chips():
        send_a(c * 2)

    @pl.when(core == 1)
    def _():
        send_a(mate)

    def piece(ref, plane, c):
        return ref.at[plane, pl.ds(pl.multiple_of(c * PIECE, 16), PIECE), :]

    load_kv.wait()

    @pl.when(me == 0)
    def _():
        @pl.loop(1, CHIPS)
        def _(c):
            pltpu.make_async_remote_copy(
                piece(own, 0, c), piece(anchor, 0, c), send_sem.at[1], recv_sem.at[1],
                device_id=at_hst(c * 2), device_id_type=MESH,
            ).start()
            pltpu.make_async_remote_copy(
                piece(own, 1, c), values_piece, send_sem.at[2], recv_sem.at[9],
                device_id=at_hst(c * 2), device_id_type=MESH,
            ).start()

        pltpu.make_async_remote_copy(
            piece(own, 1, 0), piece(anchor, 1, 0), send_sem.at[2], recv_sem.at[1],
            device_id=at_hst(1), device_id_type=MESH,
        ).start()

        @pl.loop(1, CHIPS)
        def _(c):
            pltpu.make_async_remote_copy(
                piece(own, 0, 0), piece(anchor, 0, 0), send_sem.at[3], recv_sem.at[2],
                device_id=at_hst(c * 2), device_id_type=MESH,
            ).start()

        pltpu.make_async_remote_copy(
            own.at[0], anchor.at[0], send_sem.at[4], recv_sem.at[3],
            device_id=at_hst(1), device_id_type=MESH,
        ).start()

    load_cq.wait()
    for h in range(HEADS):
        own_head(h)

    def landed(ref, n, sem):
        pltpu.make_async_copy(ref.at[pl.ds(0, n)], ref.at[pl.ds(0, n)], sem).wait()

    hand_over = pltpu.make_async_remote_copy(
        gather_q, handed_q, send_sem.at[9], recv_sem.at[8],
        device_id=at_hst(mate), device_id_type=MESH,
    )

    @pl.when(core == 0)
    def _():
        landed(gather_q, HST - 1, recv_sem.at[0])
        hand_over.start()
        rows_q[...] = gather_q[...].astype(jnp.float32).reshape(HST * 8, HD)

    @pl.when(core == 1)
    def _():
        hand_over.wait_recv()
        rows_q[...] = handed_q[...].astype(jnp.float32).reshape(HST * 8, HD)

    load_len.wait()
    q_all = jnp.concatenate(
        [rows_q[pl.ds(h, QN, stride=HEADS), :] for h in range(HEADS)], axis=0
    ).astype(jnp.bfloat16)
    load_qkv.wait()
    for plane in range(2):
        tiny = qkv[plane, :, pl.ds(kv_off, HD)].astype(jnp.float32)
        selfkv[plane] = jnp.concatenate(
            [tiny, jnp.zeros((HD - 2, HD), jnp.float32)], axis=0
        ).astype(jnp.bfloat16)
    own_len = lengths[me]
    s_ctx = dot_t(q_all, own[0])
    s_ctx = jnp.where(
        lax.broadcasted_iota(jnp.int32, s_ctx.shape, 1) < own_len, s_ctx, MASKED
    )
    s_self = dot_t(q_all, selfkv[0])
    token = lax.rem(lax.broadcasted_iota(jnp.int32, s_self.shape, 0), QN)
    key = lax.broadcasted_iota(jnp.int32, s_self.shape, 1)
    s_self = jnp.where((key < 2) & (me * 2 + key <= token), s_self, MASKED)
    peak = jnp.maximum(
        jnp.max(s_ctx, axis=1, keepdims=True), jnp.max(s_self, axis=1, keepdims=True)
    )
    peak = (peak * SCALE2).astype(jnp.bfloat16).astype(jnp.float32)
    p_ctx = jnp.exp2(s_ctx * SCALE2 - peak).astype(jnp.bfloat16)
    p_self = jnp.exp2(s_self * SCALE2 - peak).astype(jnp.bfloat16)
    o = dot(p_ctx, with_ones(own[1])) + dot(p_self, with_ones(selfkv[1]))
    lane = lax.broadcasted_iota(jnp.int32, (HEADS * QN, HD), 1)
    stats = jnp.where(lane < HD // 2, jnp.broadcast_to(peak, (HEADS * QN, HD)), o[:, HD:])
    sent_b[...] = jnp.concatenate(
        [o[:, :HD].reshape(CHIPS, 16, HD), stats.reshape(CHIPS, 16, HD)], axis=1
    ).astype(jnp.bfloat16)

    def send_b(c):
        pltpu.make_async_remote_copy(
            sent_b.at[c], got_b.at[me], send_sem.at[5], recv_sem.at[4],
            device_id=at_hst(c * 2 + 1), device_id_type=MESH,
        ).start()

    for c in other_chips():
        send_b(c)

    @pl.when(core == 0)
    def _():
        send_b(chip)

    @pl.when(core == 1)
    def _():
        got_b[pl.ds(me, 1)] = sent_b[pl.ds(chip, 1)]

    @pl.when((me > 0) & (core == 0))
    def _():
        pltpu.make_async_copy(values_piece, values_piece, recv_sem.at[9]).wait()
        pltpu.make_async_remote_copy(
            values_piece, piece(anchor, 1, chip), send_sem.at[1], recv_sem.at[1],
            device_id=at_hst(mate), device_id_type=MESH,
        ).start()

    @pl.when(me > 0)
    def _():
        pltpu.make_async_copy(
            piece(anchor, 0, 0), piece(anchor, 0, 0), recv_sem.at[1]
        ).wait()

        @pl.loop(1, CHIPS)
        def _(k):
            c = lax.rem(chip + k, CHIPS)

            @pl.when(c * 2 + core > 0)
            def _():
                pltpu.make_async_remote_copy(
                    piece(anchor, core, chip), piece(anchor, core, chip),
                    send_sem.at[3], recv_sem.at[2],
                    device_id=at_hst(c * 2 + core), device_id_type=MESH,
                ).start()

    def send_c(d):
        pltpu.make_async_remote_copy(
            att.at[chip], att.at[chip], send_sem.at[6], recv_sem.at[5],
            device_id=at_hst(d), device_id_type=MESH,
        ).start()

    @pl.when(core == 1)
    def _():
        pltpu.make_async_copy(
            got_b.at[pl.ds(0, HST - 1)], got_b.at[pl.ds(0, HST - 1)], recv_sem.at[4]
        ).wait()
        terms = got_b[...].astype(jnp.float32)
        value, stat = terms[:, :16], terms[:, 16:]
        turned = pltpu.roll(stat, HD // 2, 2)
        low = lax.broadcasted_iota(jnp.int32, stat.shape, 2) < HD // 2
        peaks = jnp.where(low, stat, turned)
        sums = jnp.where(low, turned, stat)
        factor = jnp.exp2(peaks - jnp.max(peaks, axis=0, keepdims=True))
        attended = jnp.sum(factor * value, axis=0) / jnp.sum(factor * sums, axis=0)
        att[pl.ds(chip, 1)] = attended.astype(jnp.bfloat16)[None]

        for c in other_chips():
            send_c(c * 2 + 1)
        for c in other_chips():
            send_c(c * 2)
        send_c(mate)

    @pl.when(me > 0)
    def _():
        pltpu.make_async_copy(
            anchor.at[0, pl.ds(0, ROWS - PIECE)], anchor.at[0, pl.ds(0, ROWS - PIECE)], recv_sem.at[2]
        ).wait()

    @pl.when(me > 1)
    def _():
        pltpu.make_async_remote_copy(
            anchor.at[core], anchor.at[core], send_sem.at[4], recv_sem.at[3],
            device_id=at_hst(mate), device_id_type=MESH,
        ).start()

    load_w.wait()

    @pl.when(core == 0)
    def _():
        landed(att, CHIPS, recv_sem.at[5])

    @pl.when(core == 1)
    def _():
        landed(att, CHIPS - 1, recv_sem.at[5])

    rows = att[...].astype(jnp.float32).reshape(HEADS, QN, HD)
    wide = jnp.concatenate([rows[h] for h in range(HEADS)], axis=1).astype(jnp.bfloat16)
    partial = dot(wide, weight[...]).astype(jnp.bfloat16)
    for t in range(TILES):
        r, c = t // 2, t % 2
        part[t] = partial[r * 16 : r * 16 + 16, c * HD : (c + 1) * HD]

    @pl.when(core == 1)
    def _():
        pl.semaphore_wait(barrier, 2 * TP - 1)
        pl.semaphore_signal(ready.at[1], inc=1, device_id=at_hst(mate), device_id_type=MESH)

    @pl.when(core == 0)
    def _():
        pl.semaphore_wait(ready.at[1], 1)

    slot = core * TP + z
    for t in (7, 6, 0, 5, 4, 3, 2, 1):
        r = (FIRST + t) % TP

        @pl.when((core == 0) | (z != r))
        def _():
            pltpu.make_async_remote_copy(
                part.at[t], got_d.at[slot], send_sem.at[7], recv_sem.at[6],
                device_id={"hst": column, "tp": r}, device_id_type=MESH,
            ).start()

        @pl.when((core == 1) & (z == r))
        def _():
            got_d[pl.ds(slot, 1)] = part[pl.ds(t, 1)]

    @pl.when(me > 0)
    def _():
        pltpu.make_async_copy(anchor.at[0], anchor.at[0], recv_sem.at[3]).wait()

    finish_head(0)
    finish_head(1)

    def send_e(src, where):
        pltpu.make_async_remote_copy(
            src, got_e.at[tile], send_sem.at[8], recv_sem.at[7],
            device_id=where, device_id_type=MESH,
        ).start()

    @pl.when(adds)
    def _():
        landed(got_d, 2 * TP - 1, recv_sem.at[6])
        total = got_d[...].astype(jnp.float32)
        summed[...] = jnp.sum(total[:TP], axis=0).astype(jnp.bfloat16)
        got_e[pl.ds(tile, 1)] = jnp.sum(total[TP:], axis=0).astype(jnp.bfloat16)[None]
        for d in range(TP):

            @pl.when(z != d)
            def _():
                send_e(got_e.at[tile], {"hst": column, "tp": d})

            send_e(summed, {"hst": column - 1, "tp": d})

    finish_head(2)
    finish_head(3)

    @pl.when(adds)
    def _():
        landed(got_e, TILES - 1, recv_sem.at[7])

    @pl.when(jnp.logical_not(adds))
    def _():
        landed(got_e, TILES, recv_sem.at[7])

    for t in range(TILES):
        query_out[t // 2 * 16 : t // 2 * 16 + 16, t % 2 * HD : (t % 2 + 1) * HD] = got_e[t]

    @pl.when(core == 0)
    def _():
        landed(gather_q, CHIPS - 1, send_sem.at[0])
        hand_over.wait_send()
        landed(sent_b, CHIPS, send_sem.at[5])
        landed(part, TILES, send_sem.at[7])

    @pl.when(core == 1)
    def _():
        landed(gather_q, CHIPS, send_sem.at[0])
        landed(sent_b, CHIPS - 1, send_sem.at[5])
        landed(got_d, 2 * CHIPS - 1, send_sem.at[6])

    @pl.when(adds)
    def _():
        landed(part, TILES - 1, send_sem.at[7])
        landed(got_d, 2 * TP - 1, send_sem.at[8])

    @pl.when((core == 1) & (tile >= TILES))
    def _():
        landed(part, TILES, send_sem.at[7])

    def sent(sem, rows):
        ref = own.at[0, pl.ds(0, rows)]
        pltpu.make_async_copy(ref, ref, send_sem.at[sem]).wait()

    @pl.when(me == 0)
    def _():
        sent(1, ROWS - PIECE)
        sent(2, ROWS)

    @pl.when((me > 0) & (core == 0))
    def _():
        sent(1, PIECE)

    @pl.when(core + (me == 0) > 0)
    def _():
        sent(3, ROWS - PIECE)

    @pl.when(core + (me == 0) == 0)
    def _():
        sent(3, ROWS - 2 * PIECE)

    @pl.when((me == 0) | (me > 1))
    def _():
        sent(4, ROWS)


def save(ctx_in, query_in, ctx_out, query_out, sems):
    copies = (
        pltpu.make_async_copy(ctx_in, ctx_out, sems.at[0]),
        pltpu.make_async_copy(query_in, query_out, sems.at[1]),
    )
    for copy in copies:
        copy.start()
    for copy in copies:
        copy.wait()


def per_device(ctx_q, ctx_kv, lengths, query_q, query_kv, out_weight):
    bf16, f32 = jnp.bfloat16, jnp.float32
    hbm = pl.BlockSpec(memory_space=pltpu.HBM)
    vmem = pl.BlockSpec(memory_space=pltpu.VMEM)
    outs = pl.pallas_call(
        kernel,
        out_shape=(
            pltpu.VMEM((ROWS, HEADS * HD), bf16),
            pltpu.VMEM((QN, COLS), bf16),
        ),
        in_specs=[hbm] * 6,
        out_specs=(vmem, vmem),
        scratch_shapes=[
            pltpu.SMEM((HST,), jnp.int32),
            pltpu.VMEM((ROWS, HEADS * HD), bf16),
            pltpu.VMEM((2, ROWS, HD), bf16),
            pltpu.VMEM((2, ROWS, HD), bf16),
            pltpu.VMEM((PIECE, HD), bf16),
            pltpu.VMEM((HEADS * HD, COLS), bf16),
            pltpu.VMEM((2, HEADS * HD), bf16),
            pltpu.VMEM((2, 2, KVH * HD), bf16),
            pltpu.VMEM((2, HD, HD), bf16),
            pltpu.VMEM((HEADS, ROWS, HD), f32),
            pltpu.VMEM((HEADS, ROWS, HD), f32),
            pltpu.VMEM((HEADS, ROWS, HD), f32),
            pltpu.VMEM((HST, 8, HD), bf16),
            pltpu.VMEM((HST, 8, HD), bf16),
            pltpu.VMEM((HST * 8, HD), f32),
            pltpu.VMEM((CHIPS, 32, HD), bf16),
            pltpu.VMEM((HST, 32, HD), bf16),
            pltpu.VMEM((CHIPS, 16, HD), bf16),
            pltpu.VMEM((TILES, 16, HD), bf16),
            pltpu.VMEM((2 * TP, 16, HD), bf16),
            pltpu.VMEM((16, HD), bf16),
            pltpu.VMEM((TILES, 16, HD), bf16),
            pltpu.SemaphoreType.DMA((7,)),
            pltpu.SemaphoreType.DMA((10,)),
            pltpu.SemaphoreType.DMA((10,)),
            pltpu.SemaphoreType.REGULAR((2,)),
        ],
        compiler_params=pltpu.CompilerParams(
            collective_id=0, has_side_effects=True, vmem_limit_bytes=48 * 1024 * 1024
        ),
    )(*(pltpu.with_memory_space_constraint(a, pltpu.HBM) for a in (lengths, ctx_q, ctx_kv, query_q, query_kv, out_weight)))


    any_space = pl.BlockSpec(memory_space=pl.ANY)
    return pl.pallas_call(
        save,
        out_shape=(
            jax.ShapeDtypeStruct((ROWS, HEADS * HD), bf16),
            jax.ShapeDtypeStruct((QN, COLS), bf16),
        ),
        in_specs=[any_space] * 2,
        out_specs=(any_space, any_space),
        scratch_shapes=[pltpu.SemaphoreType.DMA((2,))],
    )(*(pltpu.with_memory_space_constraint(a, pltpu.VMEM) for a in outs))


def solution(mesh):
    return jax.shard_map(
        per_device,
        mesh=mesh,
        in_specs=(
            P("hst", "tp"),
            P(None, "hst", None),
            P(),
            P("hst", "tp"),
            P(None, "hst", None),
            P("tp", "hst"),
        ),
        out_specs=(P("hst", "tp"), P(None, "hst")),
        check_vma=False,
    )
```

```python
import jax
import jax.numpy as jnp
from jax import lax
from jax.experimental import pallas as pl
from jax.experimental.pallas import tpu as pltpu
from jax.sharding import PartitionSpec as P

H = 64
KVH = 8
HD = 128
HST = 32
TP = 16
ROWS = 768
HEADS = H // TP
TILE = 256
CHIPS = HST // 2
PIECE = ROWS // CHIPS
QN = 64
COLS = 256
MASKED = -1e30
SCALE2 = HD ** (-0.5) * 1.4426950408889634
MESH = pl.DeviceIdType.MESH


SLOTS = sorted(
    [(y, x) for y in range(4) for x in range(4)],
    key=lambda o: min(o[0], 4 - o[0]) + min(o[1], 4 - o[1]),
)
CHIP_OFFSETS = SLOTS[:0:-1]
GROUPS = ((0, 5), (5, 11), (11, 16))
A_SEMS = (0, 9, 10)
TILES = 8
ADDERS = (10, 11, 12, 13, 14, 15, 1, 2)
HIGH = 10
LOW = 1


def dot_t(a, b):
    return lax.dot_general(a, b, (((1,), (1,)), ((), ())), preferred_element_type=jnp.float32)


def dot(a, b):
    return jnp.dot(a, b, preferred_element_type=jnp.float32)


def with_ones(values):
    return jnp.concatenate([values, jnp.ones_like(values)], axis=1)


def kernel(
    lengths_hbm,
    ctx_q,
    ctx_kv,
    query_q,
    query_kv,
    out_weight,
    ctx_out,
    query_out,
    lengths,
    cq,
    own,
    anchor,
    weight,
    qq,
    qkv,
    selfkv,
    out1,
    sum1,
    max1,
    gather_q,
    rows_f,
    sent_b,
    got_b,
    att,
    part,
    got_d,
    summed,
    got_e,
    local_sem,
    send_sem,
    recv_sem,
    ready,
):
    me = lax.axis_index("hst")
    z = lax.axis_index("tp")
    chip = me // 2
    core = lax.rem(me, 2)
    kv_off = pl.multiple_of((z // 2) * HD, HD)

    py, px = chip // 4, lax.rem(chip, 4)

    mate = me + 1 - 2 * core
    column = chip * 2 + 1
    tile = jnp.where(z >= HIGH, z - HIGH, z - LOW + TP - HIGH)
    chosen = (z >= HIGH) | ((z >= LOW) & (z < LOW + TILES - TP + HIGH))
    adds = (core == 1) & chosen

    def chip_at(dy, dx):
        return lax.rem(py + dy + 4, 4) * 4 + lax.rem(px + dx + 4, 4)

    def other_chips():
        for dy, dx in CHIP_OFFSETS:
            yield chip_at(dy, dx)

    def at_hst(d):
        return {"hst": d}

    load_kv = pltpu.make_async_copy(ctx_kv.at[:, :, pl.ds(kv_off, HD)], own, local_sem.at[0])
    load_cq = pltpu.make_async_copy(ctx_q, cq, local_sem.at[1])
    load_qq = pltpu.make_async_copy(query_q, qq, local_sem.at[2])
    load_qkv = pltpu.make_async_copy(query_kv, qkv, local_sem.at[3])
    load_w = pltpu.make_async_copy(out_weight, weight, local_sem.at[4])
    load_len = pltpu.make_async_copy(lengths_hbm, lengths, local_sem.at[6])
    load_qq.start()

    barrier = pltpu.get_barrier_semaphore()

    def greet(**where):
        pl.semaphore_signal(barrier, inc=1, device_id=where, device_id_type=MESH)

    for c in other_chips():
        greet(hst=c * 2)
    greet(hst=mate)
    for copy in (load_kv, load_cq, load_len, load_qkv, load_w):
        copy.start()
    for dz in (8, 7, 9, 6, 10, 5, 11, 4, 12, 3, 13, 2, 14, 1, 15):
        greet(hst=column, tp=lax.rem(z + dz, TP))

    diag_row = lax.broadcasted_iota(jnp.int32, (TILE, TILE), 0)
    diag_col = lax.broadcasted_iota(jnp.int32, (TILE, TILE), 1)

    def own_head(h):
        cols = pl.ds(pl.multiple_of(h * HD, HD), HD)
        for rb in range(ROWS // TILE):
            rows = pl.ds(rb * TILE, TILE)
            q = cq[rows, cols]
            keys = (rb + 1) * TILE
            s = dot_t(q, own[0, 0:keys, :])
            last = jnp.where(diag_col <= diag_row, s[:, keys - TILE :], MASKED)
            s = last if rb == 0 else jnp.concatenate([s[:, : keys - TILE], last], axis=1)
            m = jnp.max(s, axis=1, keepdims=True) * SCALE2
            p = jnp.exp2(s * SCALE2 - m).astype(jnp.bfloat16)
            o = dot(p, with_ones(own[1, 0:keys, :]))
            out1[h, rows, :] = o[:, :HD]
            sum1[h, rows, :] = o[:, HD:]
            max1[h, rows, :] = jnp.broadcast_to(m, (TILE, HD))

    def live(rb, value):
        own_len = lengths[me]
        rid = rb * TILE + lax.broadcasted_iota(jnp.int32, (TILE, HD), 0)
        return jnp.where(rid < own_len, value, 0.0).astype(jnp.bfloat16)

    def anchor_head(h):
        cols = pl.ds(pl.multiple_of(h * HD, HD), HD)
        for rb in range(ROWS // TILE):
            rows = pl.ds(rb * TILE, TILE)
            q = cq[rows, cols]
            s = dot_t(q, anchor[0])
            before = max1[h, rows, :]
            m = jnp.maximum(jnp.max(s, axis=1, keepdims=True) * SCALE2, before[:, :1])
            p = jnp.exp2(s * SCALE2 - m).astype(jnp.bfloat16)
            o = dot(p, with_ones(anchor[1]))
            keep = jnp.exp2(before - m)
            num = out1[h, rows, :] * keep + o[:, :HD]
            den = sum1[h, rows, :] * keep + o[:, HD:]
            ctx_out[rows, cols] = live(rb, num / den)

    def first_head(h):
        cols = pl.ds(pl.multiple_of(h * HD, HD), HD)
        for rb in range(ROWS // TILE):
            rows = pl.ds(rb * TILE, TILE)
            ctx_out[rows, cols] = live(rb, out1[h, rows, :] / sum1[h, rows, :])

    def finish_head(h):
        @pl.when(me > 0)
        def _():
            anchor_head(h)

        @pl.when(me == 0)
        def _():
            first_head(h)

    load_qq.wait()
    mine = qq[...].astype(jnp.float32)
    gather_q[pl.ds(core, 1)] = jnp.concatenate(
        [mine[t : t + 1, h * HD : (h + 1) * HD] for t in range(2) for h in range(HEADS)], axis=0
    ).astype(jnp.bfloat16)[None]

    @pl.when(core == 0)
    def _():
        pl.semaphore_wait(barrier, HST - 1)
        pl.semaphore_signal(ready.at[0], inc=1, device_id=at_hst(mate), device_id_type=MESH)

    @pl.when(core == 1)
    def _():
        pl.semaphore_wait(ready.at[0], 1)

    def send_a(d, k, group):
        pltpu.make_async_remote_copy(
            gather_q.at[core], gather_q.at[2 * k + core], send_sem.at[0],
            recv_sem.at[A_SEMS[group]], device_id=at_hst(d), device_id_type=MESH,
        ).start()

    for group in (2, 1, 0):
        for k in reversed(range(*GROUPS[group])):
            if k:
                send_a(chip_at(*SLOTS[k]) * 2, k, group)
                send_a(chip_at(*SLOTS[k]) * 2 + 1, k, group)
    send_a(mate, 0, 0)

    def piece(ref, plane, c):
        return ref.at[plane, pl.ds(pl.multiple_of(c * PIECE, 16), PIECE), :]

    load_kv.wait()

    @pl.when(me == 0)
    def _():
        @pl.loop(1, CHIPS)
        def _(c):
            pltpu.make_async_remote_copy(
                piece(own, 0, c), piece(anchor, 0, c), send_sem.at[1], recv_sem.at[1],
                device_id=at_hst(c * 2), device_id_type=MESH,
            ).start()
            pltpu.make_async_remote_copy(
                piece(own, 1, c), piece(anchor, 1, c), send_sem.at[2], recv_sem.at[1],
                device_id=at_hst(c * 2 + 1), device_id_type=MESH,
            ).start()

        pltpu.make_async_remote_copy(
            piece(own, 1, 0), piece(anchor, 1, 0), send_sem.at[2], recv_sem.at[1],
            device_id=at_hst(1), device_id_type=MESH,
        ).start()

        @pl.loop(1, CHIPS)
        def _(c):
            pltpu.make_async_remote_copy(
                piece(own, 0, 0), piece(anchor, 0, 0), send_sem.at[3], recv_sem.at[2],
                device_id=at_hst(c * 2), device_id_type=MESH,
            ).start()

        pltpu.make_async_remote_copy(
            own.at[0], anchor.at[0], send_sem.at[4], recv_sem.at[3],
            device_id=at_hst(1), device_id_type=MESH,
        ).start()

    load_cq.wait()
    first = jnp.where(me == 0, 0, 2)
    pl.loop(0, first)(own_head)

    def landed(ref, n, sem):
        pltpu.make_async_copy(ref.at[pl.ds(0, n)], ref.at[pl.ds(0, n)], sem).wait()

    load_len.wait()
    load_qkv.wait()
    for plane in range(2):
        tiny = qkv[plane, :, pl.ds(kv_off, HD)].astype(jnp.float32)
        selfkv[plane] = jnp.concatenate(
            [tiny, jnp.zeros((HD - 2, HD), jnp.float32)], axis=0
        ).astype(jnp.bfloat16)
    own_len = lengths[me]
    quarter = lax.shift_right_logical(lax.broadcasted_iota(jnp.int32, (16, HD), 0), 2)

    def query_terms(lo, hi):
        n = (hi - lo) * 16
        q = gather_q[2 * lo : 2 * hi].astype(jnp.float32).reshape(n, HD).astype(jnp.bfloat16)
        s_ctx = dot_t(q, own[0])
        s_ctx = jnp.where(
            lax.broadcasted_iota(jnp.int32, s_ctx.shape, 1) < own_len, s_ctx, MASKED
        )
        s_self = dot_t(q, selfkv[0])
        token = jnp.concatenate(
            [chip_at(-SLOTS[k][0], -SLOTS[k][1]) * 4 + quarter for k in range(lo, hi)], axis=0
        )
        key = lax.broadcasted_iota(jnp.int32, s_self.shape, 1)
        s_self = jnp.where((key < 2) & (me * 2 + key <= token), s_self, MASKED)
        peak = jnp.maximum(
            jnp.max(s_ctx, axis=1, keepdims=True), jnp.max(s_self, axis=1, keepdims=True)
        )
        peak = (peak * SCALE2).astype(jnp.bfloat16).astype(jnp.float32)
        p_ctx = jnp.exp2(s_ctx * SCALE2 - peak).astype(jnp.bfloat16)
        p_self = jnp.exp2(s_self * SCALE2 - peak).astype(jnp.bfloat16)
        o = dot(p_ctx, with_ones(own[1])) + dot(p_self, with_ones(selfkv[1]))
        lane = lax.broadcasted_iota(jnp.int32, (n, HD), 1)
        stats = jnp.where(lane < HD // 2, jnp.broadcast_to(peak, (n, HD)), o[:, HD:])
        sent_b[lo:hi] = jnp.concatenate(
            [o[:, :HD].reshape(hi - lo, 16, HD), stats.reshape(hi - lo, 16, HD)], axis=1
        ).astype(jnp.bfloat16)

    def send_b(k, d):
        pltpu.make_async_remote_copy(
            sent_b.at[k], got_b.at[me], send_sem.at[5], recv_sem.at[4],
            device_id=at_hst(d), device_id_type=MESH,
        ).start()

    for group, (lo, hi) in enumerate(GROUPS):
        landed(gather_q, 2 * (hi - lo) - (group == 0), recv_sem.at[A_SEMS[group]])
        query_terms(lo, hi)
        for k in range(lo, hi):
            dy, dx = SLOTS[k]
            if k < CHIPS - 1:
                send_b(k, chip_at(2 - dy, 2 - dx) * 2 + 1)

    @pl.when(core == 0)
    def _():
        send_b(CHIPS - 1, mate)

    @pl.when(core == 1)
    def _():
        got_b[pl.ds(me, 1)] = sent_b[CHIPS - 1 : CHIPS]

    pl.loop(first, HEADS)(own_head)
    opposite = chip_at(2, 2)

    def send_c(d):
        pltpu.make_async_remote_copy(
            att.at[opposite], att.at[opposite], send_sem.at[6], recv_sem.at[5],
            device_id=at_hst(d), device_id_type=MESH,
        ).start()

    @pl.when(core == 1)
    def _():
        pltpu.make_async_copy(
            got_b.at[pl.ds(0, HST - 1)], got_b.at[pl.ds(0, HST - 1)], recv_sem.at[4]
        ).wait()
        terms = got_b[...].astype(jnp.float32)
        value, stat = terms[:, :16], terms[:, 16:]
        turned = pltpu.roll(stat, HD // 2, 2)
        low = lax.broadcasted_iota(jnp.int32, stat.shape, 2) < HD // 2
        peaks = jnp.where(low, stat, turned)
        sums = jnp.where(low, turned, stat)
        factor = jnp.exp2(peaks - jnp.max(peaks, axis=0, keepdims=True))
        attended = jnp.sum(factor * value, axis=0) / jnp.sum(factor * sums, axis=0)
        att[pl.ds(opposite, 1)] = attended.astype(jnp.bfloat16)[None]

        for c in other_chips():
            send_c(c * 2 + 1)
        for c in other_chips():
            send_c(c * 2)
        send_c(mate)

    @pl.when(me > 0)
    def _():
        pltpu.make_async_copy(
            piece(anchor, 0, 0), piece(anchor, 0, 0), recv_sem.at[1]
        ).wait()

        @pl.loop(1, CHIPS)
        def _(k):
            c = lax.rem(chip + k, CHIPS)

            @pl.when(c * 2 + core > 0)
            def _():
                pltpu.make_async_remote_copy(
                    piece(anchor, core, chip), piece(anchor, core, chip),
                    send_sem.at[3], recv_sem.at[2],
                    device_id=at_hst(c * 2 + core), device_id_type=MESH,
                ).start()

    load_w.wait()

    @pl.when(core == 0)
    def _():
        landed(att, CHIPS, recv_sem.at[5])

    @pl.when(core == 1)
    def _():
        landed(att, CHIPS - 1, recv_sem.at[5])

    rows_f[...] = att[...].astype(jnp.float32).reshape(HST * 8, HD)
    wide = jnp.concatenate(
        [rows_f[pl.ds(h, QN, stride=HEADS), :] for h in range(HEADS)], axis=1
    ).astype(jnp.bfloat16)
    partial = dot(wide, weight[...]).astype(jnp.bfloat16)
    for t in range(TILES):
        r, c = t // 2, t % 2
        part[t] = partial[r * 16 : r * 16 + 16, c * HD : (c + 1) * HD]

    @pl.when(core == 1)
    def _():
        pl.semaphore_wait(barrier, 2 * TP - 1)
        pl.semaphore_signal(ready.at[1], inc=1, device_id=at_hst(mate), device_id_type=MESH)

    @pl.when(core == 0)
    def _():
        pl.semaphore_wait(ready.at[1], 1)

    for t in (7, 6, 0, 5, 4, 3, 2, 1):
        r = ADDERS[t]

        @pl.when((core == 0) | (z != r))
        def _():
            pltpu.make_async_remote_copy(
                part.at[t], got_d.at[core, z], send_sem.at[7], recv_sem.at[6 + core],
                device_id={"hst": column, "tp": r}, device_id_type=MESH,
            ).start()

        @pl.when((core == 1) & (z == r))
        def _():
            got_d[1, pl.ds(z, 1)] = part[pl.ds(t, 1)]

    @pl.when(me > 0)
    def _():
        pltpu.make_async_copy(
            anchor.at[0, pl.ds(0, ROWS - PIECE)], anchor.at[0, pl.ds(0, ROWS - PIECE)], recv_sem.at[2]
        ).wait()

    @pl.when(me > 1)
    def _():
        pltpu.make_async_remote_copy(
            anchor.at[core], anchor.at[core], send_sem.at[4], recv_sem.at[3],
            device_id=at_hst(mate), device_id_type=MESH,
        ).start()

    @pl.when(me > 0)
    def _():
        pltpu.make_async_copy(anchor.at[0], anchor.at[0], recv_sem.at[3]).wait()

    early = jnp.where(z < TP // 2, HEADS, 0)
    pl.loop(0, early)(finish_head)

    def send_e(src, d, core_to):
        pltpu.make_async_remote_copy(
            src, got_e.at[tile], send_sem.at[8], recv_sem.at[8],
            device_id={"hst": column - 1 + core_to, "tp": d}, device_id_type=MESH,
        ).start()

    @pl.when(adds)
    def _():
        landed(got_d.at[1], TP - 1, recv_sem.at[7])
        total = jnp.sum(got_d[1].astype(jnp.float32), axis=0)
        got_e[pl.ds(tile, 1)] = total.astype(jnp.bfloat16)[None]
        for d in range(TP):

            @pl.when(z != d)
            def _():
                send_e(got_e.at[tile], d, 1)

        landed(got_d.at[0], TP, recv_sem.at[6])
        total = jnp.sum(got_d[0].astype(jnp.float32), axis=0)
        summed[...] = total.astype(jnp.bfloat16)
        for d in range(TP):
            send_e(summed, d, 0)

    pl.loop(early, HEADS)(finish_head)

    @pl.when(adds)
    def _():
        landed(got_e, TILES - 1, recv_sem.at[8])

    @pl.when(jnp.logical_not(adds))
    def _():
        landed(got_e, TILES, recv_sem.at[8])

    for t in range(TILES):
        query_out[t // 2 * 16 : t // 2 * 16 + 16, t % 2 * HD : (t % 2 + 1) * HD] = got_e[t]

    landed(gather_q, HST - 1, send_sem.at[0])
    @pl.when(core == 0)
    def _():
        landed(sent_b, CHIPS, send_sem.at[5])
        landed(part, TILES, send_sem.at[7])

    @pl.when(core == 1)
    def _():
        landed(sent_b, CHIPS - 1, send_sem.at[5])
        landed(got_d.at[0], TP, send_sem.at[6])
        landed(got_d.at[0], TP - 1, send_sem.at[6])

    @pl.when(adds)
    def _():
        landed(part, TILES - 1, send_sem.at[7])
        landed(got_d.at[0], TP, send_sem.at[8])
        landed(got_d.at[0], TP - 1, send_sem.at[8])

    @pl.when((core == 1) & jnp.logical_not(chosen))
    def _():
        landed(part, TILES, send_sem.at[7])

    def sent(sem, rows):
        ref = own.at[0, pl.ds(0, rows)]
        pltpu.make_async_copy(ref, ref, send_sem.at[sem]).wait()

    @pl.when(me == 0)
    def _():
        sent(1, ROWS - PIECE)
        sent(2, ROWS)

    @pl.when(core + (me == 0) > 0)
    def _():
        sent(3, ROWS - PIECE)

    @pl.when(core + (me == 0) == 0)
    def _():
        sent(3, ROWS - 2 * PIECE)

    @pl.when((me == 0) | (me > 1))
    def _():
        sent(4, ROWS)


def save(ctx_in, query_in, ctx_out, query_out, sems):
    copies = (
        pltpu.make_async_copy(ctx_in, ctx_out, sems.at[0]),
        pltpu.make_async_copy(query_in, query_out, sems.at[1]),
    )
    for copy in copies:
        copy.start()
    for copy in copies:
        copy.wait()


def per_device(ctx_q, ctx_kv, lengths, query_q, query_kv, out_weight):
    bf16, f32 = jnp.bfloat16, jnp.float32
    hbm = pl.BlockSpec(memory_space=pltpu.HBM)
    vmem = pl.BlockSpec(memory_space=pltpu.VMEM)
    outs = pl.pallas_call(
        kernel,
        out_shape=(
            pltpu.VMEM((ROWS, HEADS * HD), bf16),
            pltpu.VMEM((QN, COLS), bf16),
        ),
        in_specs=[hbm] * 6,
        out_specs=(vmem, vmem),
        scratch_shapes=[
            pltpu.SMEM((HST,), jnp.int32),
            pltpu.VMEM((ROWS, HEADS * HD), bf16),
            pltpu.VMEM((2, ROWS, HD), bf16),
            pltpu.VMEM((2, ROWS, HD), bf16),
            pltpu.VMEM((HEADS * HD, COLS), bf16),
            pltpu.VMEM((2, HEADS * HD), bf16),
            pltpu.VMEM((2, 2, KVH * HD), bf16),
            pltpu.VMEM((2, HD, HD), bf16),
            pltpu.VMEM((HEADS, ROWS, HD), f32),
            pltpu.VMEM((HEADS, ROWS, HD), f32),
            pltpu.VMEM((HEADS, ROWS, HD), f32),
            pltpu.VMEM((HST, 8, HD), bf16),
            pltpu.VMEM((HST * 8, HD), f32),
            pltpu.VMEM((CHIPS, 32, HD), bf16),
            pltpu.VMEM((HST, 32, HD), bf16),
            pltpu.VMEM((CHIPS, 16, HD), bf16),
            pltpu.VMEM((TILES, 16, HD), bf16),
            pltpu.VMEM((2, TP, 16, HD), bf16),
            pltpu.VMEM((16, HD), bf16),
            pltpu.VMEM((TILES, 16, HD), bf16),
            pltpu.SemaphoreType.DMA((7,)),
            pltpu.SemaphoreType.DMA((10,)),
            pltpu.SemaphoreType.DMA((11,)),
            pltpu.SemaphoreType.REGULAR((2,)),
        ],
        compiler_params=pltpu.CompilerParams(
            collective_id=0, has_side_effects=True, vmem_limit_bytes=48 * 1024 * 1024
        ),
    )(*(pltpu.with_memory_space_constraint(a, pltpu.HBM) for a in (lengths, ctx_q, ctx_kv, query_q, query_kv, out_weight)))


    any_space = pl.BlockSpec(memory_space=pl.ANY)
    return pl.pallas_call(
        save,
        out_shape=(
            jax.ShapeDtypeStruct((ROWS, HEADS * HD), bf16),
            jax.ShapeDtypeStruct((QN, COLS), bf16),
        ),
        in_specs=[any_space] * 2,
        out_specs=(any_space, any_space),
        scratch_shapes=[pltpu.SemaphoreType.DMA((2,))],
    )(*(pltpu.with_memory_space_constraint(a, pltpu.VMEM) for a in outs))


def solution(mesh):
    return jax.shard_map(
        per_device,
        mesh=mesh,
        in_specs=(
            P("hst", "tp"),
            P(None, "hst", None),
            P(),
            P("hst", "tp"),
            P(None, "hst", None),
            P("tp", "hst"),
        ),
        out_specs=(P("hst", "tp"), P(None, "hst")),
        check_vma=False,
    )
```

```python
import jax
import jax.numpy as jnp
from jax import lax
from jax.experimental import pallas as pl
from jax.experimental.pallas import tpu as pltpu
from jax.sharding import PartitionSpec as P

H = 64
KVH = 8
HD = 128
HST = 32
TP = 16
ROWS = 768
HEADS = H // TP
TILE = 256
CHIPS = HST // 2
PIECE = ROWS // CHIPS
QN = 64
COLS = 256
MASKED = -1e30
SCALE2 = HD ** (-0.5) * 1.4426950408889634
MESH = pl.DeviceIdType.MESH


SLOTS = sorted(
    [(y, x) for y in range(4) for x in range(4)],
    key=lambda o: min(o[0], 4 - o[0]) + min(o[1], 4 - o[1]),
)
CHIP_OFFSETS = SLOTS[:0:-1]
GROUPS = ((0, 5), (5, 11), (11, 16))
A_SEMS = (0, 9, 10)
TILES = 8
ADDERS = (11, 12, 13, 14, 15, 0, 1, 2)
HIGH = 11
LOW = 0


def dot_t(a, b):
    return lax.dot_general(a, b, (((1,), (1,)), ((), ())), preferred_element_type=jnp.float32)


def dot(a, b):
    return jnp.dot(a, b, preferred_element_type=jnp.float32)


def with_ones(values):
    return jnp.concatenate([values, jnp.ones_like(values)], axis=1)


def kernel(
    lengths_hbm,
    ctx_q,
    ctx_kv,
    query_q,
    query_kv,
    out_weight,
    ctx_out,
    query_out,
    lengths,
    cq,
    own,
    anchor,
    weight,
    qq,
    qkv,
    selfkv,
    out1,
    sum1,
    max1,
    gather_q,
    rows_f,
    sent_b,
    got_b,
    att,
    part,
    got_d,
    summed,
    got_e,
    local_sem,
    send_sem,
    recv_sem,
    ready,
):
    me = lax.axis_index("hst")
    z = lax.axis_index("tp")
    chip = me // 2
    core = lax.rem(me, 2)
    kv_off = pl.multiple_of((z // 2) * HD, HD)

    py, px = chip // 4, lax.rem(chip, 4)

    mate = me + 1 - 2 * core
    column = chip * 2 + 1
    tile = jnp.where(z >= HIGH, z - HIGH, z - LOW + TP - HIGH)
    chosen = (z >= HIGH) | ((z >= LOW) & (z < LOW + TILES - TP + HIGH))
    adds = (core == 1) & chosen

    def chip_at(dy, dx):
        return lax.rem(py + dy + 4, 4) * 4 + lax.rem(px + dx + 4, 4)

    def other_chips():
        for dy, dx in CHIP_OFFSETS:
            yield chip_at(dy, dx)

    def at_hst(d):
        return {"hst": d}

    load_kv = pltpu.make_async_copy(ctx_kv.at[:, :, pl.ds(kv_off, HD)], own, local_sem.at[0])
    load_cq = pltpu.make_async_copy(ctx_q, cq, local_sem.at[1])
    load_qq = pltpu.make_async_copy(query_q, qq, local_sem.at[2])
    load_qkv = pltpu.make_async_copy(query_kv, qkv, local_sem.at[3])
    load_w = pltpu.make_async_copy(out_weight, weight, local_sem.at[4])
    load_len = pltpu.make_async_copy(lengths_hbm, lengths, local_sem.at[6])
    load_qq.start()

    barrier = pltpu.get_barrier_semaphore()

    def greet(**where):
        pl.semaphore_signal(barrier, inc=1, device_id=where, device_id_type=MESH)

    for c in other_chips():
        greet(hst=c * 2)
    greet(hst=mate)
    for copy in (load_kv, load_cq, load_len, load_qkv, load_w):
        copy.start()
    for dz in (8, 7, 9, 6, 10, 5, 11, 4, 12, 3, 13, 2, 14, 1, 15):
        greet(hst=column, tp=lax.rem(z + dz, TP))

    diag_row = lax.broadcasted_iota(jnp.int32, (TILE, TILE), 0)
    diag_col = lax.broadcasted_iota(jnp.int32, (TILE, TILE), 1)

    def own_head(h):
        cols = pl.ds(pl.multiple_of(h * HD, HD), HD)
        for rb in range(ROWS // TILE):
            rows = pl.ds(rb * TILE, TILE)
            q = cq[rows, cols]
            keys = (rb + 1) * TILE
            s = dot_t(q, own[0, 0:keys, :])
            last = jnp.where(diag_col <= diag_row, s[:, keys - TILE :], MASKED)
            s = last if rb == 0 else jnp.concatenate([s[:, : keys - TILE], last], axis=1)
            m = jnp.max(s, axis=1, keepdims=True) * SCALE2
            p = jnp.exp2(s * SCALE2 - m).astype(jnp.bfloat16)
            o = dot(p, with_ones(own[1, 0:keys, :]))
            out1[h, rows, :] = o[:, :HD]
            sum1[h, rows, :] = o[:, HD:]
            max1[h, rows, :] = jnp.broadcast_to(m, (TILE, HD))

    def live(rb, value):
        own_len = lengths[me]
        rid = rb * TILE + lax.broadcasted_iota(jnp.int32, (TILE, HD), 0)
        return jnp.where(rid < own_len, value, 0.0).astype(jnp.bfloat16)

    def anchor_head(h):
        cols = pl.ds(pl.multiple_of(h * HD, HD), HD)
        for rb in range(ROWS // TILE):
            rows = pl.ds(rb * TILE, TILE)
            q = cq[rows, cols]
            s = dot_t(q, anchor[0])
            before = max1[h, rows, :]
            m = jnp.maximum(jnp.max(s, axis=1, keepdims=True) * SCALE2, before[:, :1])
            p = jnp.exp2(s * SCALE2 - m).astype(jnp.bfloat16)
            o = dot(p, with_ones(anchor[1]))
            keep = jnp.exp2(before - m)
            num = out1[h, rows, :] * keep + o[:, :HD]
            den = sum1[h, rows, :] * keep + o[:, HD:]
            ctx_out[rows, cols] = live(rb, num / den)

    def first_head(h):
        cols = pl.ds(pl.multiple_of(h * HD, HD), HD)
        for rb in range(ROWS // TILE):
            rows = pl.ds(rb * TILE, TILE)
            ctx_out[rows, cols] = live(rb, out1[h, rows, :] / sum1[h, rows, :])

    def finish_head(h):
        @pl.when(me > 0)
        def _():
            anchor_head(h)

        @pl.when(me == 0)
        def _():
            first_head(h)

    load_qq.wait()
    mine = qq[...].astype(jnp.float32)
    gather_q[pl.ds(core, 1)] = jnp.concatenate(
        [mine[t : t + 1, h * HD : (h + 1) * HD] for t in range(2) for h in range(HEADS)], axis=0
    ).astype(jnp.bfloat16)[None]

    @pl.when(core == 0)
    def _():
        pl.semaphore_wait(barrier, HST - 1)
        pl.semaphore_signal(ready.at[0], inc=1, device_id=at_hst(mate), device_id_type=MESH)

    @pl.when(core == 1)
    def _():
        pl.semaphore_wait(ready.at[0], 1)

    def send_a(d, k, group):
        pltpu.make_async_remote_copy(
            gather_q.at[core], gather_q.at[2 * k + core], send_sem.at[0],
            recv_sem.at[A_SEMS[group]], device_id=at_hst(d), device_id_type=MESH,
        ).start()

    for group in (2, 0, 1):
        for k in reversed(range(*GROUPS[group])):
            if k:
                send_a(chip_at(*SLOTS[k]) * 2, k, group)
                send_a(chip_at(*SLOTS[k]) * 2 + 1, k, group)
    send_a(mate, 0, 0)

    def piece(ref, plane, c):
        return ref.at[plane, pl.ds(pl.multiple_of(c * PIECE, 16), PIECE), :]

    load_kv.wait()

    @pl.when(me == 0)
    def _():
        @pl.loop(1, CHIPS)
        def _(c):
            pltpu.make_async_remote_copy(
                piece(own, 0, c), piece(anchor, 0, c), send_sem.at[1], recv_sem.at[1],
                device_id=at_hst(c * 2), device_id_type=MESH,
            ).start()
            pltpu.make_async_remote_copy(
                piece(own, 1, c), piece(anchor, 1, c), send_sem.at[2], recv_sem.at[1],
                device_id=at_hst(c * 2 + 1), device_id_type=MESH,
            ).start()

        pltpu.make_async_remote_copy(
            piece(own, 1, 0), piece(anchor, 1, 0), send_sem.at[2], recv_sem.at[1],
            device_id=at_hst(1), device_id_type=MESH,
        ).start()

        @pl.loop(1, CHIPS)
        def _(c):
            pltpu.make_async_remote_copy(
                piece(own, 0, 0), piece(anchor, 0, 0), send_sem.at[3], recv_sem.at[2],
                device_id=at_hst(c * 2), device_id_type=MESH,
            ).start()

        pltpu.make_async_remote_copy(
            own.at[0], anchor.at[0], send_sem.at[4], recv_sem.at[3],
            device_id=at_hst(1), device_id_type=MESH,
        ).start()

    load_cq.wait()
    first = jnp.where(me == 0, 0, 1)
    pl.loop(0, first)(own_head)

    def landed(ref, n, sem):
        pltpu.make_async_copy(ref.at[pl.ds(0, n)], ref.at[pl.ds(0, n)], sem).wait()

    load_len.wait()
    load_qkv.wait()
    for plane in range(2):
        tiny = qkv[plane, :, pl.ds(kv_off, HD)].astype(jnp.float32)
        selfkv[plane] = jnp.concatenate(
            [tiny, jnp.zeros((HD - 2, HD), jnp.float32)], axis=0
        ).astype(jnp.bfloat16)
    own_len = lengths[me]
    quarter = lax.shift_right_logical(lax.broadcasted_iota(jnp.int32, (16, HD), 0), 2)

    def query_terms(lo, hi):
        n = (hi - lo) * 16
        q = gather_q[2 * lo : 2 * hi].astype(jnp.float32).reshape(n, HD).astype(jnp.bfloat16)
        s_ctx = dot_t(q, own[0])
        s_ctx = jnp.where(
            lax.broadcasted_iota(jnp.int32, s_ctx.shape, 1) < own_len, s_ctx, MASKED
        )
        s_self = dot_t(q, selfkv[0])
        token = jnp.concatenate(
            [chip_at(-SLOTS[k][0], -SLOTS[k][1]) * 4 + quarter for k in range(lo, hi)], axis=0
        )
        key = lax.broadcasted_iota(jnp.int32, s_self.shape, 1)
        s_self = jnp.where((key < 2) & (me * 2 + key <= token), s_self, MASKED)
        peak = jnp.maximum(
            jnp.max(s_ctx, axis=1, keepdims=True), jnp.max(s_self, axis=1, keepdims=True)
        )
        peak = (peak * SCALE2).astype(jnp.bfloat16).astype(jnp.float32)
        p_ctx = jnp.exp2(s_ctx * SCALE2 - peak).astype(jnp.bfloat16)
        p_self = jnp.exp2(s_self * SCALE2 - peak).astype(jnp.bfloat16)
        o = dot(p_ctx, with_ones(own[1])) + dot(p_self, with_ones(selfkv[1]))
        lane = lax.broadcasted_iota(jnp.int32, (n, HD), 1)
        stats = jnp.where(lane < HD // 2, jnp.broadcast_to(peak, (n, HD)), o[:, HD:])
        sent_b[lo:hi] = jnp.concatenate(
            [o[:, :HD].reshape(hi - lo, 16, HD), stats.reshape(hi - lo, 16, HD)], axis=1
        ).astype(jnp.bfloat16)

    def send_b(k, d):
        pltpu.make_async_remote_copy(
            sent_b.at[k], got_b.at[me], send_sem.at[5], recv_sem.at[4],
            device_id=at_hst(d), device_id_type=MESH,
        ).start()

    for group, (lo, hi) in enumerate(GROUPS):
        landed(gather_q, 2 * (hi - lo) - (group == 0), recv_sem.at[A_SEMS[group]])
        query_terms(lo, hi)
        for k in range(lo, hi):
            dy, dx = SLOTS[k]
            if k < CHIPS - 1:
                send_b(k, chip_at(2 - dy, 2 - dx) * 2 + 1)

    @pl.when(core == 0)
    def _():
        send_b(CHIPS - 1, mate)

    @pl.when(core == 1)
    def _():
        got_b[pl.ds(me, 1)] = sent_b[CHIPS - 1 : CHIPS]

    pl.loop(first, 3)(own_head)
    opposite = chip_at(2, 2)

    def send_c(d):
        pltpu.make_async_remote_copy(
            att.at[opposite], att.at[opposite], send_sem.at[6], recv_sem.at[5],
            device_id=at_hst(d), device_id_type=MESH,
        ).start()

    @pl.when(core == 1)
    def _():
        pltpu.make_async_copy(
            got_b.at[pl.ds(0, HST - 1)], got_b.at[pl.ds(0, HST - 1)], recv_sem.at[4]
        ).wait()
        terms = got_b[...].astype(jnp.float32)
        value, stat = terms[:, :16], terms[:, 16:]
        turned = pltpu.roll(stat, HD // 2, 2)
        low = lax.broadcasted_iota(jnp.int32, stat.shape, 2) < HD // 2
        peaks = jnp.where(low, stat, turned)
        sums = jnp.where(low, turned, stat)
        factor = jnp.exp2(peaks - jnp.max(peaks, axis=0, keepdims=True))
        attended = jnp.sum(factor * value, axis=0) / jnp.sum(factor * sums, axis=0)
        att[pl.ds(opposite, 1)] = attended.astype(jnp.bfloat16)[None]

        for c in other_chips():
            send_c(c * 2 + 1)
        for c in other_chips():
            send_c(c * 2)
        send_c(mate)

    own_head(3)

    @pl.when(me > 0)
    def _():
        pltpu.make_async_copy(
            piece(anchor, 0, 0), piece(anchor, 0, 0), recv_sem.at[1]
        ).wait()

        @pl.loop(1, CHIPS)
        def _(k):
            c = lax.rem(chip + k, CHIPS)

            @pl.when(c * 2 + core > 0)
            def _():
                pltpu.make_async_remote_copy(
                    piece(anchor, core, chip), piece(anchor, core, chip),
                    send_sem.at[3], recv_sem.at[2],
                    device_id=at_hst(c * 2 + core), device_id_type=MESH,
                ).start()

    load_w.wait()

    @pl.when(core == 0)
    def _():
        landed(att, CHIPS, recv_sem.at[5])

    @pl.when(core == 1)
    def _():
        landed(att, CHIPS - 1, recv_sem.at[5])

    rows_f[0 : HST * 8] = att[...].astype(jnp.float32).reshape(HST * 8, HD)
    wide = jnp.concatenate(
        [rows_f[pl.ds(h, QN, stride=HEADS), :] for h in range(HEADS)], axis=1
    ).astype(jnp.bfloat16)
    partial = dot(wide, weight[...]).astype(jnp.bfloat16)
    for t in range(TILES):
        r, c = t // 2, t % 2
        part[t] = partial[r * 16 : r * 16 + 16, c * HD : (c + 1) * HD]

    @pl.when(core == 1)
    def _():
        pl.semaphore_wait(barrier, 2 * TP - 1)
        pl.semaphore_signal(ready.at[1], inc=1, device_id=at_hst(mate), device_id_type=MESH)

    @pl.when(core == 0)
    def _():
        pl.semaphore_wait(ready.at[1], 1)

    for t in (7, 6, 0, 5, 4, 3, 2, 1):
        r = ADDERS[t]

        @pl.when((core == 0) | (z != r))
        def _():
            pltpu.make_async_remote_copy(
                part.at[t], got_d.at[core, z], send_sem.at[7], recv_sem.at[6 + core],
                device_id={"hst": column, "tp": r}, device_id_type=MESH,
            ).start()

        @pl.when((core == 1) & (z == r))
        def _():
            got_d[1, pl.ds(z, 1)] = part[pl.ds(t, 1)]

    def finish():
        @pl.when(me > 0)
        def _():
            pltpu.make_async_copy(
                anchor.at[0, pl.ds(0, ROWS - PIECE)], anchor.at[0, pl.ds(0, ROWS - PIECE)], recv_sem.at[2]
            ).wait()

        @pl.when(me > 1)
        def _():
            pltpu.make_async_remote_copy(
                anchor.at[core], anchor.at[core], send_sem.at[4], recv_sem.at[3],
                device_id=at_hst(mate), device_id_type=MESH,
            ).start()

        @pl.when(me > 0)
        def _():
            pltpu.make_async_copy(anchor.at[0], anchor.at[0], recv_sem.at[3]).wait()

        pl.loop(0, HEADS)(finish_head)

    @pl.when(z < TP // 2)
    def _():
        finish()

    def send_e(src, d, core_to):
        pltpu.make_async_remote_copy(
            src, got_e.at[tile], send_sem.at[8], recv_sem.at[8],
            device_id={"hst": column - 1 + core_to, "tp": d}, device_id_type=MESH,
        ).start()

    @pl.when(adds)
    def _():
        landed(got_d.at[1], TP - 1, recv_sem.at[7])
        total = jnp.sum(got_d[1].astype(jnp.float32), axis=0)
        got_e[pl.ds(tile, 1)] = total.astype(jnp.bfloat16)[None]
        for d in range(TP):

            @pl.when(z != d)
            def _():
                send_e(got_e.at[tile], d, 1)

        landed(got_d.at[0], TP, recv_sem.at[6])
        total = jnp.sum(got_d[0].astype(jnp.float32), axis=0)
        summed[...] = total.astype(jnp.bfloat16)
        for d in range(TP):
            send_e(summed, d, 0)

    @pl.when(z >= TP // 2)
    def _():
        finish()

    @pl.when(adds)
    def _():
        landed(got_e, TILES - 1, recv_sem.at[8])

    @pl.when(jnp.logical_not(adds))
    def _():
        landed(got_e, TILES, recv_sem.at[8])

    for t in range(TILES):
        query_out[t // 2 * 16 : t // 2 * 16 + 16, t % 2 * HD : (t % 2 + 1) * HD] = got_e[t]

    landed(gather_q, HST - 1, send_sem.at[0])
    @pl.when(core == 0)
    def _():
        landed(sent_b, CHIPS, send_sem.at[5])
        landed(part, TILES, send_sem.at[7])

    @pl.when(core == 1)
    def _():
        landed(sent_b, CHIPS - 1, send_sem.at[5])
        landed(got_d.at[0], TP, send_sem.at[6])
        landed(got_d.at[0], TP - 1, send_sem.at[6])

    @pl.when(adds)
    def _():
        landed(part, TILES - 1, send_sem.at[7])
        landed(got_d.at[0], TP, send_sem.at[8])
        landed(got_d.at[0], TP - 1, send_sem.at[8])

    @pl.when((core == 1) & jnp.logical_not(chosen))
    def _():
        landed(part, TILES, send_sem.at[7])

    def sent(sem, rows):
        ref = own.at[0, pl.ds(0, rows)]
        pltpu.make_async_copy(ref, ref, send_sem.at[sem]).wait()

    @pl.when(me == 0)
    def _():
        sent(1, ROWS - PIECE)
        sent(2, ROWS)

    @pl.when(core + (me == 0) > 0)
    def _():
        sent(3, ROWS - PIECE)

    @pl.when(core + (me == 0) == 0)
    def _():
        sent(3, ROWS - 2 * PIECE)

    @pl.when((me == 0) | (me > 1))
    def _():
        sent(4, ROWS)


def save(ctx_in, query_in, ctx_out, query_out, sems):
    copies = [pltpu.make_async_copy(query_in, query_out, sems.at[6])]
    for i in range(6):
        rows = pl.ds(i * HD, HD)
        copies.append(pltpu.make_async_copy(ctx_in.at[rows], ctx_out.at[rows], sems.at[i]))
    for copy in copies:
        copy.start()
    for copy in copies:
        copy.wait()


def per_device(ctx_q, ctx_kv, lengths, query_q, query_kv, out_weight):
    bf16, f32 = jnp.bfloat16, jnp.float32
    hbm = pl.BlockSpec(memory_space=pltpu.HBM)
    vmem = pl.BlockSpec(memory_space=pltpu.VMEM)
    outs = pl.pallas_call(
        kernel,
        out_shape=(
            pltpu.VMEM((ROWS, HEADS * HD), bf16),
            pltpu.VMEM((QN, COLS), bf16),
        ),
        in_specs=[hbm] * 6,
        out_specs=(vmem, vmem),
        scratch_shapes=[
            pltpu.SMEM((HST,), jnp.int32),
            pltpu.VMEM((ROWS, HEADS * HD), bf16),
            pltpu.VMEM((2, ROWS, HD), bf16),
            pltpu.VMEM((2, ROWS, HD), bf16),
            pltpu.VMEM((HEADS * HD, COLS), bf16),
            pltpu.VMEM((2, HEADS * HD), bf16),
            pltpu.VMEM((2, 2, KVH * HD), bf16),
            pltpu.VMEM((2, HD, HD), bf16),
            pltpu.VMEM((HEADS, ROWS, HD), f32),
            pltpu.VMEM((HEADS, ROWS, HD), f32),
            pltpu.VMEM((HEADS, ROWS, HD), f32),
            pltpu.VMEM((HST, 8, HD), bf16),
            pltpu.VMEM((HST * 8 + 8, HD), f32),
            pltpu.VMEM((CHIPS, 32, HD), bf16),
            pltpu.VMEM((HST, 32, HD), bf16),
            pltpu.VMEM((CHIPS, 16, HD), bf16),
            pltpu.VMEM((TILES, 16, HD), bf16),
            pltpu.VMEM((2, TP, 16, HD), bf16),
            pltpu.VMEM((16, HD), bf16),
            pltpu.VMEM((TILES, 16, HD), bf16),
            pltpu.SemaphoreType.DMA((7,)),
            pltpu.SemaphoreType.DMA((10,)),
            pltpu.SemaphoreType.DMA((11,)),
            pltpu.SemaphoreType.REGULAR((2,)),
        ],
        compiler_params=pltpu.CompilerParams(
            collective_id=0, has_side_effects=True, vmem_limit_bytes=48 * 1024 * 1024
        ),
    )(*(pltpu.with_memory_space_constraint(a, pltpu.HBM) for a in (lengths, ctx_q, ctx_kv, query_q, query_kv, out_weight)))


    any_space = pl.BlockSpec(memory_space=pl.ANY)
    return pl.pallas_call(
        save,
        out_shape=(
            jax.ShapeDtypeStruct((ROWS, HEADS * HD), bf16),
            jax.ShapeDtypeStruct((QN, COLS), bf16),
        ),
        in_specs=[any_space] * 2,
        out_specs=(any_space, any_space),
        scratch_shapes=[pltpu.SemaphoreType.DMA((7,))],
    )(*(pltpu.with_memory_space_constraint(a, pltpu.VMEM) for a in outs))


def solution(mesh):
    return jax.shard_map(
        per_device,
        mesh=mesh,
        in_specs=(
            P("hst", "tp"),
            P(None, "hst", None),
            P(),
            P("hst", "tp"),
            P(None, "hst", None),
            P("tp", "hst"),
        ),
        out_specs=(P("hst", "tp"), P(None, "hst")),
        check_vma=False,
    )
```
